256 devices in a mesh: dp: 16 (over x, y_hi, core), seq: 16 (over y_lo, z).
Axes of the slice: x: 4, y: 4 (y_hi: 2, y_lo: 2; y = y_hi * 2 + y_lo), z: 8, core: 2. Of those that a mesh axis runs over, the one named last changes fastest.
Arguments:
- activations: bfloat16 [16, 20480, 768], P('dp', 'seq'), may hold values from -400 to 400
- nucleotides: int32 [16, 20480], P('dp', 'seq'), may hold values from 0 to 3
- base_table: float32 [4, 768], replicated, may hold values from -4 to 4
- norm_gain: float32 [768], replicated, may hold values from 0.1 to 1.9
- filter_weight: bfloat16 [3, 768, 768], P(None, 'dp'), may hold values from -0.125 to 0.125
- upstream: bfloat16 [16, 20480, 768], P('dp', 'seq'), may hold values from -6 to 6
Outputs:
- input_grad: bfloat16 [16, 20480, 768], P('dp', 'seq')
- weight_grad: float32 [3, 768, 768], P(None, 'dp')
The draws below stay inside these ranges and needn't reach their ends.
All inputs are finite; a program needn't handle non-finite values.
Results may differ from the reference program's by a relative error of at most 0.0056.
Values may be sent and summed in bfloat16 or wider, within the bound.
No kernel may reach another device: no remote copies, remote signals or barrier semaphores. Data moves between devices by JAX's collectives and lax.ppermute only.
A program may use at most 64 MiB of HBM per device.

```python
import math
import jax
import jax.numpy as jnp
from jax import lax

C = 768
FILTER_TAPS = 3
DILATION_STEP = 32
WINDOWS = 16
LENGTH = 20480


def draw_activations(key, part):
    key = jax.random.fold_in(key, 11)
    keys = jax.random.split(key, 3)
    row_scale = jnp.exp(jax.random.uniform(keys[0], (WINDOWS, LENGTH, 1), jnp.float32, 0.0, math.log(10.0)))
    col_scale = jnp.exp(jax.random.uniform(keys[1], (1, 1, C), jnp.float32, 0.0, math.log(10.0)))
    values = jnp.clip(jax.random.normal(keys[2], (WINDOWS, LENGTH, C), jnp.float32), -4.0, 4.0)
    return (values * row_scale * col_scale).astype(jnp.bfloat16)


def place_ends(values, key, least, top_value):
    index_at = [jax.random.randint(jax.random.fold_in(key, axis), (), 0, length) for axis, length in enumerate(values.shape)]
    widest = values.shape.index(max(values.shape))
    next_to = index_at[:widest] + [(index_at[widest] + 1) % values.shape[widest]] + index_at[widest + 1:]
    return values.at[tuple(index_at)].set(least).at[tuple(next_to)].set(top_value)


def with_spikes(drawn, key, source, target, blocks, factor):
    owner, partner = [(jnp.arange(drawn.shape[axis_at]) // (drawn.shape[axis_at] // blocks)).reshape([-1 if axis == axis_at else 1 for axis in range(drawn.ndim)]) for axis_at in (source, target)]
    chosen = jax.random.permutation(key, blocks)[partner]
    strong = (owner == chosen) | (owner == (partner + blocks // 2) % blocks)
    return jnp.where(strong, factor * drawn, drawn)


def steps_of(own_key, shape, pieces, smallest, top_value):
    gain, own = 1.0, jax.random.fold_in(own_key, 6)
    for axis_at, parts in pieces:
        heights = jnp.exp(jax.random.uniform(jax.random.fold_in(own, axis_at), (parts,), jnp.float32, smallest / len(pieces), top_value / len(pieces)))
        gain = gain * jnp.repeat(heights, shape[axis_at] // parts).reshape([-1 if axis == axis_at else 1 for axis in range(len(shape))])
    return gain


def noise(key, shape, scale, most, cuts=(), kind=jnp.bfloat16):
    values = jax.random.normal(key, shape, jnp.float32) * scale
    if len(cuts) > 0:
        values = steps_of(key, shape, cuts, -0.22, 0.18) * values
    return jnp.clip(values, min=-most, max=most).astype(kind)


def gaussian_with(rng, dims, scale, reach, cuts, heavy, kind=jnp.bfloat16):
    values = scale * jax.random.normal(rng, dims, jnp.float32)
    if cuts:
        values = values * steps_of(rng, dims, cuts, -0.22, 0.18)
    return jnp.clip(with_spikes(values, jax.random.fold_in(rng, 3), *heavy), -reach, reach).astype(kind)


def setup_inputs(seed: int = 0) -> dict:
    arg_keys = jax.random.split(jax.random.key(seed), 7)
    activations = draw_activations(jax.random.fold_in(arg_keys[6], 71), 0)
    nucleotides = place_ends(jax.random.randint(arg_keys[1], (WINDOWS, LENGTH), 0, 4), jax.random.fold_in(arg_keys[1], 1), 0, 3).astype(jnp.int32)
    base_table = noise(arg_keys[2], (4, C), 1.0, 4.0, (), jnp.float32)
    norm_gain = jnp.clip(1.0 + 0.18 * jax.random.normal(arg_keys[3], (C,), jnp.float32), 0.1, 1.9)
    filter_weight = noise(arg_keys[4], (FILTER_TAPS, C, C), (FILTER_TAPS * C) ** -0.5, 0.125, ((1, 16),))
    upstream = gaussian_with(arg_keys[5], (WINDOWS, LENGTH, C), 1.0, 6.0, ((0, 16), (1, 16)), (1, 2, 16, 2.0))
    return {"activations": activations, "nucleotides": nucleotides, "base_table": base_table, "norm_gain": norm_gain, "filter_weight": filter_weight, "upstream": upstream}


def gelu_slope(value):
    coeff = math.sqrt(2.0 / math.pi)
    inner = coeff * (value + 0.044715 * value * value * value)
    tangent = jnp.tanh(inner)
    return 0.5 * (1.0 + tangent) + 0.5 * value * (1.0 - tangent * tangent) * coeff * (1.0 + 3.0 * 0.044715 * value * value)

def reference(activations, nucleotides, base_table, norm_gain, filter_weight, upstream):
    receptive_reach = DILATION_STEP * (FILTER_TAPS // 2)
    table = base_table.astype(jnp.float32)

    def window(carry, items):
        tokens, bases, incoming = items
        hot = (bases[:, None] == jnp.arange(4, dtype=jnp.int32)[None, :]).astype(jnp.float32)
        inputs = tokens.astype(jnp.float32) + jnp.dot(hot, table, precision=lax.Precision.HIGHEST)
        scale_inv = lax.rsqrt(lax.optimization_barrier(jnp.mean(inputs * inputs, axis=-1, keepdims=True)) + 1e-06)
        normed = (inputs * scale_inv * norm_gain).astype(jnp.bfloat16)
        padded_input = jnp.pad(normed, ((receptive_reach, receptive_reach), (0, 0)))
        element_count = normed.shape[0]
        convolve_block = jnp.zeros((element_count, C), jnp.float32)
        for filter_tap in range(FILTER_TAPS):
            convolve_block = convolve_block + jnp.dot(padded_input[filter_tap * DILATION_STEP:filter_tap * DILATION_STEP + element_count], filter_weight[filter_tap], preferred_element_type=jnp.float32)
        backward_pass = (incoming.astype(jnp.float32) * gelu_slope(convolve_block)).astype(jnp.bfloat16)
        back_pad = jnp.pad(backward_pass, ((receptive_reach, receptive_reach), (0, 0)))
        normed_grad = jnp.zeros((element_count, C), jnp.float32)
        gradient_list = []
        for filter_tap in range(FILTER_TAPS):
            start_offset = (FILTER_TAPS - 1 - filter_tap) * DILATION_STEP
            normed_grad = normed_grad + lax.dot_general(back_pad[start_offset:start_offset + element_count], filter_weight[filter_tap], (((1,), (1,)), ((), ())), preferred_element_type=jnp.float32)
            gradient_list.append(lax.dot_general(padded_input[filter_tap * DILATION_STEP:filter_tap * DILATION_STEP + element_count], backward_pass, (((0,), (0,)), ((), ())), preferred_element_type=jnp.float32))
        scaled = norm_gain * normed_grad
        spread = lax.optimization_barrier(jnp.mean(scaled * inputs, axis=-1, keepdims=True))
        result = incoming.astype(jnp.float32) + scale_inv * scaled - inputs * scale_inv * scale_inv * scale_inv * spread
        return (carry + jnp.stack(gradient_list), result.astype(jnp.bfloat16))
    start_grad = jnp.zeros((FILTER_TAPS, C, C), jnp.float32)
    total, input_grad = lax.scan(window, start_grad, (activations, nucleotides, upstream))
    weight_grad = total / math.sqrt(WINDOWS * LENGTH)
    return (input_grad, weight_grad)
```

```python
import functools
import math

import jax
import jax.numpy as jnp
from jax import lax
from jax.experimental import pallas as pl
from jax.experimental.pallas import tpu as pltpu
from jax.sharding import Mesh, PartitionSpec as P

FILTER_TAPS = 3
DILATION_STEP = 32
REACH = 32
AXES = ("x", "yh", "core", "yl", "z")
SIZES = (4, 2, 2, 2, 8)
SEQ = ("yl", "z")
RING_Y = ("yh", "yl")
BF16 = jnp.bfloat16
F32 = jnp.float32


def shift(value, axis, count, step):
    pairs = [(i, (i + step) % count) for i in range(count)]
    return lax.ppermute(value, axis, pairs)


def swap(value, axis, count, mask):
    return lax.ppermute(value, axis, [(i, i ^ mask) for i in range(count)])


def gelu_slope(value):
    coeff = math.sqrt(2.0 / math.pi)
    square = value * value
    tangent = jnp.tanh(value * (coeff + coeff * 0.044715 * square))
    return (0.5 + 0.5 * tangent) * (
        1.0 + value * (1.0 - tangent) * (coeff + coeff * 3.0 * 0.044715 * square)
    )


def gather_weight(weight, x, yh, core):
    half = weight.shape[2] // 2
    mine = lax.dynamic_slice_in_dim(weight, core * half, half, axis=2)
    other = lax.dynamic_slice_in_dim(weight, (1 - core) * half, half, axis=2)
    arrived = swap(other, "core", 2, 1)
    own = jnp.where(
        core == 0,
        jnp.concatenate([mine, arrived], axis=1),
        jnp.concatenate([arrived, mine], axis=1),
    )
    rows = weight.shape[1]
    across = swap(own, RING_Y, 4, 3)
    up_own = shift(own, "x", 4, 1)
    down_own = shift(own, "x", 4, -1)
    up_across = shift(across, "x", 4, 1)
    down_across = shift(across, "x", 4, -1)
    far = [
        shift(up_own[:, :rows], "x", 4, 1),
        shift(down_own[:, rows:], "x", 4, -1),
        shift(up_across[:, :rows], "x", 4, 1),
        shift(down_across[:, rows:], "x", 4, -1),
    ]
    return [own, across, up_own, up_across, down_own, down_across] + far


def forward_kernel(position, *refs):
    pieces, refs = refs[:10], refs[10:]
    normed_hbm, turned_hbm, upstream_hbm = refs[0:2], refs[2:4], refs[4:6]
    weight_out, back_out, grad_out = refs[6], refs[7:9], refs[9:12]
    weight, normed, turned, upstream, back, grad = refs[12:18]
    piece_sem, normed_sem, turned_sem, upstream_sem, back_sem, grad_sem, weight_sem = refs[18:]
    x, yh = position[0], position[1]
    wide = pieces[0].shape[1]
    rows = wide // 2

    def at(step_x, step_y, low):
        place = ((x + step_x) % 4) * (2 * wide) + ((yh + step_y) % 2) * wide + low
        return pl.multiple_of(place, 16)

    places = [at(0, 0, 0), at(0, 1, 0), at(3, 0, 0), at(3, 1, 0), at(1, 0, 0), at(1, 1, 0)]
    places += [at(2, 0, 0), at(2, 0, rows), at(2, 1, 0), at(2, 1, rows)]
    copies = []
    for index, (piece, place) in enumerate(zip(pieces, places)):
        copies.append(
            pltpu.make_async_copy(
                piece, weight.at[:, pl.ds(place, piece.shape[1]), :], piece_sem.at[index]
            )
        )
    loads = []
    for index in range(2):
        loads.append(
            (
                pltpu.make_async_copy(normed_hbm[index], normed.at[index], normed_sem.at[index]),
                pltpu.make_async_copy(
                    upstream_hbm[index], upstream.at[index], upstream_sem.at[index]
                ),
                pltpu.make_async_copy(turned_hbm[index], turned.at[index], turned_sem.at[index]),
            )
        )
    for copy in copies:
        copy.start()
    for load in loads:
        load[0].start()
        load[1].start()
    for load in loads:
        load[2].start()
    for copy in copies:
        copy.wait()
    save = pltpu.make_async_copy(weight, weight_out, weight_sem)
    save.start()
    length = back.shape[1]
    block = length // 3
    back_saves = []
    for index in range(2):
        loads[index][0].wait()
        loads[index][1].wait()
        for start in range(0, length, block):
            conv = jnp.zeros((block, weight.shape[2]), F32)
            for tap in range(FILTER_TAPS):
                low = start + tap * DILATION_STEP
                conv = conv + jnp.dot(
                    normed[index, low : low + block, :], weight[tap], preferred_element_type=F32
                )
            incoming = upstream[index, start : start + block, :].astype(F32)
            back[index, start : start + block, :] = (incoming * gelu_slope(conv)).astype(BF16)
        back_save = pltpu.make_async_copy(back.at[index], back_out[index], back_sem.at[index])
        back_save.start()
        back_saves.append(back_save)
    for load in loads:
        load[2].wait()
    count = turned.shape[2]
    saves = []
    for tap in range(FILTER_TAPS):
        low = 2 * REACH - tap * DILATION_STEP
        total = jnp.dot(turned[0], back[0, low : low + count, :], preferred_element_type=F32)
        total = total + jnp.dot(
            turned[1], back[1, low : low + count, :], preferred_element_type=F32
        )
        grad[tap] = total.astype(BF16)
        grad_save = pltpu.make_async_copy(grad.at[tap], grad_out[tap], grad_sem.at[tap])
        grad_save.start()
        saves.append(grad_save)
    for copy in [save] + back_saves + saves:
        copy.wait()


def forward(position, pieces, normed, turned, upstream):
    channels = normed[0].shape[1]
    half = channels // 2
    length = upstream[0].shape[0]
    count = turned[0].shape[1]
    anywhere = pl.BlockSpec(memory_space=pl.ANY)
    dma = pltpu.SemaphoreType.DMA
    return pl.pallas_call(
        forward_kernel,
        out_shape=[jax.ShapeDtypeStruct((FILTER_TAPS, channels, half), BF16)]
        + [jax.ShapeDtypeStruct((length, half), BF16)] * 2
        + [jax.ShapeDtypeStruct((channels, half), BF16)] * 3,
        in_specs=[pl.BlockSpec(memory_space=pltpu.SMEM)] + [anywhere] * 16,
        out_specs=[anywhere] * 6,
        scratch_shapes=[
            pltpu.VMEM((FILTER_TAPS, channels, half), BF16),
            pltpu.VMEM((2,) + normed[0].shape, BF16),
            pltpu.VMEM((2,) + turned[0].shape, BF16),
            pltpu.VMEM((2, length, half), BF16),
            pltpu.VMEM((2, length, half), BF16),
            pltpu.VMEM((FILTER_TAPS, channels, half), BF16),
            dma((10,)),
            dma((2,)),
            dma((2,)),
            dma((2,)),
            dma((2,)),
            dma((3,)),
            dma,
        ],
        compiler_params=pltpu.CompilerParams(vmem_limit_bytes=56 * 1024 * 1024),
        name="forward",
    )(position, *pieces, *normed, *turned, *upstream)


def backward_kernel(back_a, back_b, weight_a, weight_b, inputs, scale, gain, incoming, out):
    block = out.shape[0]
    start = pl.program_id(0) * block
    grad = jnp.zeros(out.shape, F32)
    for back, weight in ((back_a, weight_a), (back_b, weight_b)):
        for tap in range(FILTER_TAPS):
            low = start + (FILTER_TAPS - 1 - tap) * DILATION_STEP
            grad = grad + lax.dot_general(
                back[pl.ds(pl.multiple_of(low, 32), block), :],
                weight[tap],
                (((1,), (1,)), ((), ())),
                preferred_element_type=F32,
            )
    scaled = grad * gain[...]
    value = inputs[...]
    factor = scale[...]
    spread = jnp.mean(scaled * value, axis=-1, keepdims=True)
    result = incoming[...].astype(F32) + factor * scaled - value * (factor * factor * factor * spread)
    out[...] = result.astype(BF16)


def backward(back, weight, inputs, scale, gain, incoming):
    count, channels = inputs.shape
    block = 256
    whole = lambda array: pl.BlockSpec(array.shape, lambda i: (0,) * array.ndim)
    part = pl.BlockSpec((block, channels), lambda i: (i, 0))
    return pl.pallas_call(
        backward_kernel,
        grid=(count // block,),
        out_shape=jax.ShapeDtypeStruct((count, channels), BF16),
        in_specs=[whole(back[0]), whole(back[1]), whole(weight[0]), whole(weight[1]), part]
        + [pl.BlockSpec((block, 1), lambda i: (i, 0)), whole(gain), part],
        out_specs=part,
        compiler_params=pltpu.CompilerParams(vmem_limit_bytes=56 * 1024 * 1024),
        name="backward",
    )(*back, *weight, inputs, scale, gain, incoming)


def reduce_weight_grad(grads, x, y):
    quarter = grads[0].shape[0] // 4
    rows = quarter // 4

    def along_x(step):
        start = ((x + step) % 4) * quarter
        return jnp.stack(
            [lax.dynamic_slice_in_dim(grad, start, quarter, axis=0) for grad in grads[:2]]
        )

    def along_y(step):
        start = ((y + step) % 4) * rows
        tall = grads[2].reshape(4, quarter, -1)
        return lax.dynamic_slice_in_dim(tall, start, rows, axis=1)

    first = [along_x(0)] + [shift(along_x(step), "x", 4, step) for step in (1, 3, 2)]
    second = [along_y(0)] + [shift(along_y(step), RING_Y, 4, step) for step in (1, 3, 2)]

    def over_y(step):
        start = ((y + step) % 4) * rows
        return sum(
            lax.dynamic_slice_in_dim(part, start, rows, axis=1).astype(F32) for part in first
        )

    def over_x(step):
        start = (x + step) % 4
        return sum(
            lax.dynamic_slice_in_dim(part, start, 1, axis=0).astype(F32) for part in second
        )

    total_y = over_y(0) + sum(
        shift(over_y(step).astype(BF16), RING_Y, 4, step).astype(F32) for step in (1, 3, 2)
    )
    total_x = over_x(0) + sum(
        shift(over_x(step).astype(BF16), "x", 4, step).astype(F32) for step in (1, 3, 2)
    )
    return jnp.concatenate([total_y, total_x], axis=0)


def share_weight_grad(total, yl, core):
    for mask in (1, 2, 4):
        sent = total.astype(BF16)
        total = sent.astype(F32) + swap(sent, "z", 8, mask).astype(F32)
    mine = total.astype(BF16)
    other = swap(mine, "yl", 2, 1)
    by_core = [jnp.where(yl == rows, mine, other) for rows in range(2)]
    kept = jnp.where(core == 0, by_core[0], by_core[1])
    sent = jnp.where(core == 0, by_core[1], by_core[0])
    arrived = swap(sent, "core", 2, 1)
    low = jnp.where(core == 0, kept, arrived)
    high = jnp.where(core == 0, arrived, kept)
    return jnp.concatenate([low, high], axis=2).astype(F32)


def on_device(activations, nucleotides, base_table, norm_gain, filter_weight, upstream):
    x, yh, core, yl = (lax.axis_index(name) for name in ("x", "yh", "core", "yl"))
    pieces = gather_weight(filter_weight, x, yh, core)
    tokens = activations[0]
    count, channels = tokens.shape
    half = channels // 2
    bases = nucleotides[0][:, None]
    row = base_table[3][None]
    for base in (2, 1, 0):
        row = jnp.where(bases == base, base_table[base][None], row)
    inputs = tokens.astype(F32) + row
    scale_inv = lax.rsqrt(jnp.mean(inputs * inputs, axis=-1, keepdims=True) + 1e-06)
    normed = (inputs * scale_inv * norm_gain).astype(BF16)
    incoming = upstream[0]
    last = jnp.concatenate([normed[count - 2 * REACH :], incoming[count - REACH :]])
    first = jnp.concatenate([normed[: 2 * REACH], incoming[:REACH]])
    low = lax.ppermute(last, SEQ, [(i, i + 1) for i in range(15)])
    high = lax.ppermute(first, SEQ, [(i + 1, i) for i in range(15)])
    normed_wide = jnp.concatenate([low[: 2 * REACH], normed, high[: 2 * REACH]])
    upstream_wide = jnp.concatenate([low[2 * REACH :], incoming, high[2 * REACH :]])
    upstream_mine = lax.dynamic_slice_in_dim(upstream_wide, core * half, half, axis=1)
    upstream_sent = lax.dynamic_slice_in_dim(upstream_wide, (1 - core) * half, half, axis=1)
    normed_other = swap(normed_wide, "core", 2, 1)
    upstream_other = swap(upstream_sent, "core", 2, 1)
    turned = normed.T
    turned_other = swap(turned, "core", 2, 1)
    position = jnp.stack([x, yh]).astype(jnp.int32)
    weight, back, back_other, *grads = forward(
        position,
        pieces,
        (normed_wide, normed_other),
        (turned, turned_other),
        (upstream_mine, upstream_other),
    )
    total = reduce_weight_grad(grads, x, yh * 2 + yl)
    back_rest = swap(back_other, "core", 2, 1)
    weight_rest = swap(weight, "core", 2, 1)
    result = backward(
        (back, back_rest), (weight, weight_rest), inputs, scale_inv, norm_gain[None], incoming
    )
    weight_grad = share_weight_grad(total, yl, core)
    total_rows = 16 * 16 * count
    return (result[None], weight_grad / math.sqrt(total_rows))


def solution(mesh):
    grid = Mesh(mesh.devices.reshape(SIZES), AXES)
    dp, seq = ("x", "yh", "core"), SEQ
    in_specs = (
        P(dp, seq, None),
        P(dp, seq),
        P(),
        P(),
        P(None, dp, None),
        P(dp, seq, None),
    )
    out_specs = (P(dp, seq, None), P(None, dp, None))
    return jax.shard_map(
        on_device, mesh=grid, in_specs=in_specs, out_specs=out_specs, check_vma=False
    )
```

```python
import functools
import math

import jax
import jax.numpy as jnp
from jax import lax
from jax.experimental import pallas as pl
from jax.experimental.pallas import tpu as pltpu
from jax.sharding import Mesh, PartitionSpec as P

FILTER_TAPS = 3
DILATION_STEP = 32
REACH = 32
AXES = ("x", "yh", "core", "yl", "z")
SIZES = (4, 2, 2, 2, 8)
SEQ = ("yl", "z")
RING_Y = ("yh", "yl")
BF16 = jnp.bfloat16
F32 = jnp.float32


def shift(value, axis, count, step):
    pairs = [(i, (i + step) % count) for i in range(count)]
    return lax.ppermute(value, axis, pairs)


def swap(value, axis, count, mask):
    return lax.ppermute(value, axis, [(i, i ^ mask) for i in range(count)])


def gelu_slope(value):
    coeff = math.sqrt(2.0 / math.pi)
    square = value * value
    tangent = jnp.tanh(value * (coeff + coeff * 0.044715 * square))
    return (0.5 + 0.5 * tangent) * (
        1.0 + value * (1.0 - tangent) * (coeff + coeff * 3.0 * 0.044715 * square)
    )


def join(*arrays):
    return lax.optimization_barrier(arrays)


def load_weight(position, pieces, weight, sem):
    x, yh, core = position[0], position[1], position[2]
    rows = pieces[0].shape[2]
    steps = [(0, 0), (0, 1), (3, 0), (3, 1), (1, 0), (1, 1)]
    parts = []
    for piece, step in zip(pieces[:6], steps):
        parts += [(piece.at[0], step, 0), (piece.at[1], step, 1)]
    far = [((2, 0), 0), ((2, 0), 1), ((2, 1), 0), ((2, 1), 1)]
    parts += [(piece, step, side) for piece, (step, side) in zip(pieces[6:], far)]
    copies = []
    for index, (part, (step_x, step_y), side) in enumerate(parts):
        owner = ((x + step_x) % 4) * 4 + ((yh + step_y) % 2) * 2 + (core + side) % 2
        place = pl.multiple_of(owner * rows, 16)
        copies.append(
            pltpu.make_async_copy(part, weight.at[:, pl.ds(place, rows), :], sem.at[index])
        )
    return copies


def forward_kernel(position, *refs):
    pieces, refs = refs[:10], refs[10:]
    normed_hbm, edge_hbm, upstream_hbm = refs[0:2], refs[2:6], refs[6:8]
    weight_out, back_out = refs[8], refs[9:11]
    weight, normed, upstream, back = refs[11:15]
    piece_sem, load_sem, back_sem, weight_sem = refs[15:]
    core = position[2]
    half = weight.shape[2]
    count = normed_hbm[0].shape[0]
    lane = pl.multiple_of(core * half, 128)
    copies = load_weight(position, pieces, weight, piece_sem)
    loads = []
    for index in range(2):
        low, high = edge_hbm[2 * index], edge_hbm[2 * index + 1]
        center = upstream_hbm[index]
        if index == 0:
            center = center.at[:, pl.ds(lane, half)]
        moves = [
            (low.at[: 2 * REACH], normed.at[index, : 2 * REACH]),
            (normed_hbm[index], normed.at[index, 2 * REACH : 2 * REACH + count]),
            (high.at[: 2 * REACH], normed.at[index, 2 * REACH + count :]),
            (low.at[2 * REACH :, pl.ds(lane, half)], upstream.at[index, :REACH]),
            (center, upstream.at[index, REACH : REACH + count]),
            (high.at[2 * REACH :, pl.ds(lane, half)], upstream.at[index, REACH + count :]),
        ]
        loads.append(
            [
                pltpu.make_async_copy(source, target, load_sem.at[index, place])
                for place, (source, target) in enumerate(moves)
            ]
        )
    for copy in copies + loads[0] + loads[1]:
        copy.start()
    for copy in copies:
        copy.wait()
    save = pltpu.make_async_copy(weight, weight_out, weight_sem)
    save.start()
    length = back.shape[1]
    block = length // 3
    saves = [save]
    for index in range(2):
        for copy in loads[index]:
            copy.wait()
        for start in range(0, length, block):
            conv = jnp.dot(
                normed[index, start : start + block, :], weight[0], preferred_element_type=F32
            )
            for tap in range(1, FILTER_TAPS):
                low = start + tap * DILATION_STEP
                conv = conv + jnp.dot(
                    normed[index, low : low + block, :], weight[tap], preferred_element_type=F32
                )
            incoming = upstream[index, start : start + block, :].astype(F32)
            back[index, start : start + block, :] = (incoming * gelu_slope(conv)).astype(BF16)
        back_save = pltpu.make_async_copy(back.at[index], back_out[index], back_sem.at[index])
        back_save.start()
        saves.append(back_save)
    for copy in saves:
        copy.wait()


def forward(position, pieces, normed, edges, upstream):
    count, channels = normed[0].shape
    half = channels // 2
    length = count + 2 * REACH
    anywhere = pl.BlockSpec(memory_space=pl.ANY)
    dma = pltpu.SemaphoreType.DMA
    return pl.pallas_call(
        forward_kernel,
        out_shape=[jax.ShapeDtypeStruct((FILTER_TAPS, channels, half), BF16)]
        + [jax.ShapeDtypeStruct((length, half), BF16)] * 2,
        in_specs=[pl.BlockSpec(memory_space=pltpu.SMEM)] + [anywhere] * 18,
        out_specs=[anywhere] * 3,
        scratch_shapes=[
            pltpu.VMEM((FILTER_TAPS, channels, half), BF16),
            pltpu.VMEM((2, length + 2 * REACH, channels), BF16),
            pltpu.VMEM((2, length, half), BF16),
            pltpu.VMEM((2, length, half), BF16),
            dma((16,)),
            dma((2, 6)),
            dma((2,)),
            dma,
        ],
        compiler_params=pltpu.CompilerParams(vmem_limit_bytes=56 * 1024 * 1024),
        name="forward",
    )(position, *pieces, *normed, *edges, *upstream)


def weight_grad_kernel(position, *refs):
    normed_hbm, back_hbm = refs[0:2], refs[2:4]
    along_x, along_y = refs[4:8], refs[8:12]
    normed, back, grad, normed_sem, back_sem, x_sem, y_sem = refs[12:]
    x, y = position[0], position[1] * 2 + position[3]
    count, channels = normed.shape[1:]
    half = back.shape[2]
    quarter, rows = channels // 4, channels // 16
    loads = []
    for index in range(2):
        loads.append(pltpu.make_async_copy(normed_hbm[index], normed.at[index], normed_sem.at[index]))
        loads.append(pltpu.make_async_copy(back_hbm[index], back.at[index], back_sem.at[index]))
    for copy in loads:
        copy.start()
    total = None
    for index in range(2):
        loads[2 * index].wait()
        loads[2 * index + 1].wait()
        shifted = jnp.concatenate(
            [
                back[index, 2 * REACH - tap * DILATION_STEP :][:count]
                for tap in range(FILTER_TAPS)
            ],
            axis=1,
        )
        part = lax.dot_general(
            normed[index], shifted, (((0,), (0,)), ((), ())), preferred_element_type=F32
        )
        total = part if total is None else total + part
    for tap in range(FILTER_TAPS):
        grad[tap] = total[:, tap * half : (tap + 1) * half].astype(BF16)
    saves = []
    for step in range(4):
        place = pl.multiple_of(((x + step) % 4) * quarter, 16)
        saves.append(
            pltpu.make_async_copy(
                grad.at[:2, pl.ds(place, quarter), :], along_x[step], x_sem.at[step]
            )
        )
    for step in range(4):
        for owner in range(4):
            place = pl.multiple_of(owner * quarter + ((y + step) % 4) * rows, 16)
            saves.append(
                pltpu.make_async_copy(
                    grad.at[2, pl.ds(place, rows), :],
                    along_y[step].at[owner],
                    y_sem.at[step, owner],
                )
            )
    for copy in saves:
        copy.start()
    for copy in saves:
        copy.wait()


def weight_grads(position, normed, back):
    count, channels = normed[0].shape
    length, half = back[0].shape
    quarter, rows = channels // 4, channels // 16
    anywhere = pl.BlockSpec(memory_space=pl.ANY)
    dma = pltpu.SemaphoreType.DMA
    return pl.pallas_call(
        weight_grad_kernel,
        out_shape=[jax.ShapeDtypeStruct((2, quarter, half), BF16)] * 4
        + [jax.ShapeDtypeStruct((4, rows, half), BF16)] * 4,
        in_specs=[pl.BlockSpec(memory_space=pltpu.SMEM)] + [anywhere] * 4,
        out_specs=[anywhere] * 8,
        scratch_shapes=[
            pltpu.VMEM((2, count, channels), BF16),
            pltpu.VMEM((2, length, half), BF16),
            pltpu.VMEM((FILTER_TAPS, channels, half), BF16),
            dma((2,)),
            dma((2,)),
            dma((4,)),
            dma((4, 4)),
        ],
        compiler_params=pltpu.CompilerParams(vmem_limit_bytes=56 * 1024 * 1024),
        name="weight_grads",
    )(position, *normed, *back)


def backward_kernel(back_a, back_b, weight_a, weight_b, inputs, scale, gain, incoming, out):
    block = out.shape[0]
    start = pl.program_id(0) * block
    grad = jnp.zeros(out.shape, F32)
    for back, weight in ((back_a, weight_a), (back_b, weight_b)):
        for tap in range(FILTER_TAPS):
            low = start + (FILTER_TAPS - 1 - tap) * DILATION_STEP
            grad = grad + lax.dot_general(
                back[pl.ds(pl.multiple_of(low, 32), block), :],
                weight[tap],
                (((1,), (1,)), ((), ())),
                preferred_element_type=F32,
            )
    scaled = grad * gain[...]
    value = inputs[...]
    factor = scale[...]
    spread = jnp.mean(scaled * value, axis=-1, keepdims=True)
    result = incoming[...].astype(F32) + factor * scaled - value * (factor * factor * factor * spread)
    out[...] = result.astype(BF16)


def backward(back, weight, inputs, scale, gain, incoming):
    count, channels = inputs.shape
    block = 256
    whole = lambda array: pl.BlockSpec(array.shape, lambda i: (0,) * array.ndim)
    part = pl.BlockSpec((block, channels), lambda i: (i, 0))
    return pl.pallas_call(
        backward_kernel,
        grid=(count // block,),
        out_shape=jax.ShapeDtypeStruct((count, channels), BF16),
        in_specs=[whole(back[0]), whole(back[1]), whole(weight[0]), whole(weight[1]), part]
        + [pl.BlockSpec((block, 1), lambda i: (i, 0)), whole(gain), part],
        out_specs=part,
        compiler_params=pltpu.CompilerParams(vmem_limit_bytes=56 * 1024 * 1024),
        name="backward",
    )(*back, *weight, inputs, scale, gain, incoming)


def first_sums(along_x, along_y, x, y):
    rows = along_y[0].shape[1]
    by_y = []
    by_x = []
    for step in range(4):
        start = ((y + step) % 4) * rows
        parts = [lax.dynamic_slice_in_dim(part, start, rows, axis=1) for part in along_x]
        by_y.append(sum(part.astype(F32) for part in parts))
        start = (x + step) % 4
        parts = [lax.dynamic_slice_in_dim(part, start, 1, axis=0) for part in along_y]
        by_x.append(sum(part.astype(F32) for part in parts))
    return by_y, by_x


def share_weight_grad(total, yl, core):
    for mask in (1, 2, 4):
        sent = total.astype(BF16)
        total = sent.astype(F32) + swap(sent, "z", 8, mask).astype(F32)
    mine = total.astype(BF16)
    other = swap(mine, "yl", 2, 1)
    by_core = [jnp.where(yl == rows, mine, other) for rows in range(2)]
    kept = jnp.where(core == 0, by_core[0], by_core[1])
    sent = jnp.where(core == 0, by_core[1], by_core[0])
    arrived = swap(sent, "core", 2, 1)
    low = jnp.where(core == 0, kept, arrived)
    high = jnp.where(core == 0, arrived, kept)
    return jnp.concatenate([low, high], axis=2).astype(F32)


def on_device(activations, nucleotides, base_table, norm_gain, filter_weight, upstream):
    x, yh, core, yl = (lax.axis_index(name) for name in ("x", "yh", "core", "yl"))
    y = yh * 2 + yl
    position = jnp.stack([x, yh, core, yl]).astype(jnp.int32)
    tokens, incoming = activations[0], upstream[0]
    count, channels = tokens.shape
    half = channels // 2

    mine = lax.dynamic_slice_in_dim(filter_weight, core * half, half, axis=2)
    other = lax.dynamic_slice_in_dim(filter_weight, (1 - core) * half, half, axis=2)
    own = jnp.stack([mine, swap(other, "core", 2, 1)])
    own, tokens, nucleotides, incoming = join(own, tokens, nucleotides, incoming)

    across = swap(own, RING_Y, 4, 3)
    up_own, down_own = shift(own, "x", 4, 1), shift(own, "x", 4, -1)
    bases = nucleotides[0][:, None]
    row = base_table[3][None]
    for base in (2, 1, 0):
        row = jnp.where(bases == base, base_table[base][None], row)
    inputs = tokens.astype(F32) + row
    scale_inv = lax.rsqrt(jnp.mean(inputs * inputs, axis=-1, keepdims=True) + 1e-06)
    normed = (inputs * scale_inv * norm_gain).astype(BF16)
    last = jnp.concatenate([normed[count - 2 * REACH :], incoming[count - REACH :]])
    first = jnp.concatenate([normed[: 2 * REACH], incoming[:REACH]])
    upstream_sent = lax.dynamic_slice_in_dim(incoming, (1 - core) * half, half, axis=1)
    across, up_own, down_own, normed, last, first, upstream_sent = join(
        across, up_own, down_own, normed, last, first, upstream_sent
    )

    up_across, down_across = shift(across, "x", 4, 1), shift(across, "x", 4, -1)
    far_up, far_down = shift(up_own[0], "x", 4, 1), shift(down_own[1], "x", 4, -1)
    low = lax.ppermute(last, SEQ, [(i, i + 1) for i in range(15)])
    high = lax.ppermute(first, SEQ, [(i + 1, i) for i in range(15)])
    normed_other = swap(normed, "core", 2, 1)
    upstream_other = swap(upstream_sent, "core", 2, 1)
    up_across, down_across, far_up, far_down, low, high, normed_other, upstream_other = join(
        up_across, down_across, far_up, far_down, low, high, normed_other, upstream_other
    )

    far_across_up = shift(up_across[0], "x", 4, 1)
    far_across_down = shift(down_across[1], "x", 4, -1)
    low_other, high_other = swap(low, "core", 2, 1), swap(high, "core", 2, 1)
    pieces = [own, across, up_own, up_across, down_own, down_across]
    pieces += [far_up, far_down, far_across_up, far_across_down]
    weight, back, back_other = forward(
        position,
        pieces,
        (normed, normed_other),
        (low, high, low_other, high_other),
        (incoming, upstream_other),
    )

    back_rest = swap(back_other, "core", 2, 1)
    weight_rest = swap(weight, "core", 2, 1)
    grads = weight_grads(position, (normed, normed_other), (back, back_other))
    back_rest, weight_rest, *grads = join(back_rest, weight_rest, *grads)

    along_x, along_y = [grads[0]], [grads[4]]
    for step in (1, 3, 2):
        along_x.append(shift(grads[step], "x", 4, step))
        along_y.append(shift(grads[4 + step], RING_Y, 4, step))
    result = backward(
        (back, back_rest), (weight, weight_rest), inputs, scale_inv, norm_gain[None], incoming
    )
    joined = join(result, *along_x, *along_y)
    result, along_x, along_y = joined[0], joined[1:5], joined[5:]

    by_y, by_x = first_sums(along_x, along_y, x, y)
    total_y, total_x = by_y[0], by_x[0]
    for step in (1, 3, 2):
        total_y = total_y + shift(by_y[step].astype(BF16), RING_Y, 4, step).astype(F32)
        total_x = total_x + shift(by_x[step].astype(BF16), "x", 4, step).astype(F32)
    total = jnp.concatenate([total_y, total_x], axis=0)
    weight_grad = share_weight_grad(total, yl, core)
    total_rows = 16 * 16 * count
    return (result[None], weight_grad / math.sqrt(total_rows))


def solution(mesh):
    grid = Mesh(mesh.devices.reshape(SIZES), AXES)
    dp, seq = ("x", "yh", "core"), SEQ
    in_specs = (
        P(dp, seq, None),
        P(dp, seq),
        P(),
        P(),
        P(None, dp, None),
        P(dp, seq, None),
    )
    out_specs = (P(dp, seq, None), P(None, dp, None))
    return jax.shard_map(
        on_device, mesh=grid, in_specs=in_specs, out_specs=out_specs, check_vma=False
    )
```

```python
import functools
import math

import jax
import jax.numpy as jnp
from jax import lax
from jax.experimental import pallas as pl
from jax.experimental.pallas import tpu as pltpu
from jax.sharding import Mesh, PartitionSpec as P

FILTER_TAPS = 3
DILATION_STEP = 32
REACH = 32
AXES = ("x", "yh", "core", "yl", "z")
SIZES = (4, 2, 2, 2, 8)
SEQ = ("yl", "z")
RING_Y = ("yh", "yl")
BF16 = jnp.bfloat16
F32 = jnp.float32


def shift(value, axis, count, step):
    pairs = [(i, (i + step) % count) for i in range(count)]
    return lax.ppermute(value, axis, pairs)


def swap(value, axis, count, mask):
    return lax.ppermute(value, axis, [(i, i ^ mask) for i in range(count)])


def gelu_slope(value):
    coeff = math.sqrt(2.0 / math.pi)
    square = value * value
    tangent = jnp.tanh(value * (coeff + coeff * 0.044715 * square))
    return (0.5 + 0.5 * tangent) * (
        1.0 + value * (1.0 - tangent) * (coeff + coeff * 3.0 * 0.044715 * square)
    )


def join(*arrays):
    return lax.optimization_barrier(arrays)


def load_weight(position, pieces, weight, sem):
    x, yh, core = position[0], position[1], position[2]
    rows = pieces[0].shape[2]
    own, across, up_own, up_across, down_own, down_across, far = pieces
    blocks = [(own, 0, 0), (across, 0, 1), (up_own, 3, 0), (up_across, 3, 1)]
    blocks += [(down_own, 1, 0), (down_across, 1, 1), (far.at[0], 2, 0), (far.at[1], 2, 1)]
    copies = []
    for block, step_x, step_y in blocks:
        for side in range(2):
            owner = ((x + step_x) % 4) * 4 + ((yh + step_y) % 2) * 2 + (core + side) % 2
            place = pl.multiple_of(owner * rows, 16)
            copies.append(
                pltpu.make_async_copy(
                    block.at[side], weight.at[:, pl.ds(place, rows), :], sem.at[len(copies)]
                )
            )
    return copies


def forward_kernel(position, *refs):
    pieces, refs = refs[:7], refs[7:]
    normed_hbm, edges, upstream_hbm = refs[0:2], refs[2:4], refs[4:6]
    weight_out, back_out, along_x = refs[6], refs[7:9], refs[9:13]
    weight, normed, upstream, back, grad = refs[13:18]
    piece_sem, load_sem, back_sem, weight_sem, grad_sem = refs[18:]
    x, core = position[0], position[2]
    channels, half = weight.shape[1:]
    count = normed_hbm[0].shape[0]
    lane = pl.multiple_of(core * half, 128)
    copies = load_weight(position, pieces, weight, piece_sem)
    wide = 2 * REACH
    loads = []
    for index in range(2):
        center = upstream_hbm[index]
        if index == 0:
            center = center.at[:, pl.ds(lane, half)]
        rows, lanes = slice(index * wide, (index + 1) * wide), slice(index * half, (index + 1) * half)
        moves = [
            (normed_hbm[index], normed.at[index, wide : wide + count]),
            (center, upstream.at[index, REACH : REACH + count]),
        ]
        for edge, place in zip(edges, (0, wide + count)):
            moves.append((edge.at[rows], normed.at[index, place : place + wide]))
        for edge, place in zip(edges, (0, REACH + count)):
            moves.append((edge.at[2 * wide :, lanes], upstream.at[index, place : place + REACH]))
        loads.append(
            [
                pltpu.make_async_copy(source, target, load_sem.at[index, place])
                for place, (source, target) in enumerate(moves)
            ]
        )
    for copy in copies + loads[0] + loads[1]:
        copy.start()
    for copy in copies:
        copy.wait()
    save = pltpu.make_async_copy(weight, weight_out, weight_sem)
    save.start()
    length = back.shape[1]
    block = length // 3
    saves = [save]
    for index in range(2):
        for copy in loads[index]:
            copy.wait()
        for start in range(0, length, block):
            conv = jnp.dot(
                normed[index, start : start + block, :], weight[0], preferred_element_type=F32
            )
            for tap in range(1, FILTER_TAPS):
                low = start + tap * DILATION_STEP
                conv = conv + jnp.dot(
                    normed[index, low : low + block, :], weight[tap], preferred_element_type=F32
                )
            incoming = upstream[index, start : start + block, :].astype(F32)
            back[index, start : start + block, :] = (incoming * gelu_slope(conv)).astype(BF16)
        back_save = pltpu.make_async_copy(back.at[index], back_out[index], back_sem.at[index])
        back_save.start()
        saves.append(back_save)
    total = None
    for index in range(2):
        shifted = jnp.concatenate(
            [
                back[index, wide - tap * DILATION_STEP : wide - tap * DILATION_STEP + count, :]
                for tap in range(FILTER_TAPS)
            ],
            axis=1,
        )
        part = lax.dot_general(
            normed[index, wide : wide + count, :],
            shifted,
            (((0,), (0,)), ((), ())),
            preferred_element_type=F32,
        )
        total = part if total is None else total + part
    for tap in range(FILTER_TAPS):
        grad[tap] = total[:, tap * half : (tap + 1) * half].astype(BF16)
    quarter = channels // 4
    for step in range(4):
        place = pl.multiple_of(((x + step) % 4) * quarter, 16)
        grad_save = pltpu.make_async_copy(
            grad.at[:, pl.ds(place, quarter), :], along_x[step], grad_sem.at[step]
        )
        grad_save.start()
        saves.append(grad_save)
    for copy in saves:
        copy.wait()


def forward(position, pieces, normed, edges, upstream):
    count, channels = normed[0].shape
    half = channels // 2
    length = count + 2 * REACH
    anywhere = pl.BlockSpec(memory_space=pl.ANY)
    dma = pltpu.SemaphoreType.DMA
    return pl.pallas_call(
        forward_kernel,
        out_shape=[jax.ShapeDtypeStruct((FILTER_TAPS, channels, half), BF16)]
        + [jax.ShapeDtypeStruct((length, half), BF16)] * 2
        + [jax.ShapeDtypeStruct((FILTER_TAPS, channels // 4, half), BF16)] * 4,
        in_specs=[pl.BlockSpec(memory_space=pltpu.SMEM)] + [anywhere] * 13,
        out_specs=[anywhere] * 7,
        scratch_shapes=[
            pltpu.VMEM((FILTER_TAPS, channels, half), BF16),
            pltpu.VMEM((2, length + 2 * REACH, channels), BF16),
            pltpu.VMEM((2, length, half), BF16),
            pltpu.VMEM((2, length, half), BF16),
            pltpu.VMEM((FILTER_TAPS, channels, half), BF16),
            dma((16,)),
            dma((2, 6)),
            dma((2,)),
            dma,
            dma((4,)),
        ],
        compiler_params=pltpu.CompilerParams(vmem_limit_bytes=56 * 1024 * 1024),
        name="forward",
    )(position, *pieces, *normed, *edges, *upstream)


def backward_kernel(back_a, back_b, weight_a, weight_b, inputs, scale, gain, incoming, out):
    block = out.shape[0]
    start = pl.program_id(0) * block
    grad = jnp.zeros(out.shape, F32)
    for tap in range(FILTER_TAPS):
        low = pl.multiple_of(start + (FILTER_TAPS - 1 - tap) * DILATION_STEP, 32)
        rows = pl.ds(low, block)
        grad = grad + lax.dot_general(
            jnp.concatenate([back_a[rows, :], back_b[rows, :]], axis=1),
            jnp.concatenate([weight_a[tap], weight_b[tap]], axis=1),
            (((1,), (1,)), ((), ())),
            preferred_element_type=F32,
        )
    scaled = grad * gain[...]
    value = inputs[...]
    factor = scale[...]
    spread = jnp.mean(scaled * value, axis=-1, keepdims=True)
    result = incoming[...].astype(F32) + factor * scaled - value * (factor * factor * factor * spread)
    out[...] = result.astype(BF16)


def backward(back, weight, inputs, scale, gain, incoming):
    count, channels = inputs.shape
    block = 256
    whole = lambda array: pl.BlockSpec(array.shape, lambda i: (0,) * array.ndim)
    part = pl.BlockSpec((block, channels), lambda i: (i, 0))
    return pl.pallas_call(
        backward_kernel,
        grid=(count // block,),
        out_shape=jax.ShapeDtypeStruct((count, channels), BF16),
        in_specs=[whole(back[0]), whole(back[1]), whole(weight[0]), whole(weight[1]), part]
        + [pl.BlockSpec((block, 1), lambda i: (i, 0)), whole(gain), part],
        out_specs=part,
        compiler_params=pltpu.CompilerParams(vmem_limit_bytes=56 * 1024 * 1024),
        name="backward",
    )(*back, *weight, inputs, scale, gain, incoming)


def share_weight_grad(total, yl, core):
    for mask in (1, 2, 4):
        sent = total.astype(BF16)
        total = sent.astype(F32) + swap(sent, "z", 8, mask).astype(F32)
    mine = total.astype(BF16)
    other = swap(mine, "yl", 2, 1)
    by_core = [jnp.where(yl == rows, mine, other) for rows in range(2)]
    kept = jnp.where(core == 0, by_core[0], by_core[1])
    sent = jnp.where(core == 0, by_core[1], by_core[0])
    arrived = swap(sent, "core", 2, 1)
    low = jnp.where(core == 0, kept, arrived)
    high = jnp.where(core == 0, arrived, kept)
    return jnp.concatenate([low, high], axis=2).astype(F32)


def on_device(activations, nucleotides, base_table, norm_gain, filter_weight, upstream):
    x, yh, core, yl = (lax.axis_index(name) for name in ("x", "yh", "core", "yl"))
    y = yh * 2 + yl
    position = jnp.stack([x, yh, core, yl]).astype(jnp.int32)
    tokens, incoming = activations[0], upstream[0]
    count, channels = tokens.shape
    half = channels // 2

    mine = lax.dynamic_slice_in_dim(filter_weight, core * half, half, axis=2)
    other = lax.dynamic_slice_in_dim(filter_weight, (1 - core) * half, half, axis=2)
    own = jnp.stack([mine, swap(other, "core", 2, 1)])
    own, tokens, nucleotides, incoming = join(own, tokens, nucleotides, incoming)

    across = swap(own, RING_Y, 4, 3)
    up_own, down_own = shift(own, "x", 4, 1), shift(own, "x", 4, -1)
    bases = nucleotides[0][:, None]
    row = base_table[3][None]
    for base in (2, 1, 0):
        row = jnp.where(bases == base, base_table[base][None], row)
    inputs = tokens.astype(F32) + row
    scale_inv = lax.rsqrt(jnp.mean(inputs * inputs, axis=-1, keepdims=True) + 1e-06)
    normed = (inputs * scale_inv * norm_gain).astype(BF16)
    across, up_own, down_own, normed, incoming = join(across, up_own, down_own, normed, incoming)

    far = shift(jnp.stack([own, across]), "x", 4, 2)
    up_across, down_across = shift(across, "x", 4, 1), shift(across, "x", 4, -1)
    upstream_sent = lax.dynamic_slice_in_dim(incoming, (1 - core) * half, half, axis=1)
    normed_other = swap(normed, "core", 2, 1)
    upstream_other = swap(upstream_sent, "core", 2, 1)

    def edge(rows, reach_rows):
        upstream_edge = lax.dynamic_slice_in_dim(incoming[reach_rows], core * half, half, axis=1)
        upstream_edge = jnp.concatenate([upstream_edge, upstream_other[reach_rows]], axis=1)
        return jnp.concatenate([normed[rows], normed_other[rows], upstream_edge])

    low = lax.ppermute(
        edge(slice(count - 2 * REACH, count), slice(count - REACH, count)),
        SEQ,
        [(i, i + 1) for i in range(15)],
    )
    high = lax.ppermute(
        edge(slice(0, 2 * REACH), slice(0, REACH)), SEQ, [(i + 1, i) for i in range(15)]
    )
    weight, back, back_other, *grads = forward(
        position,
        [own, across, up_own, up_across, down_own, down_across, far],
        (normed, normed_other),
        (low, high),
        (incoming, upstream_other),
    )

    back_rest = swap(back_other, "core", 2, 1)
    weight_rest = swap(weight, "core", 2, 1)
    along_x = [grads[0]] + [shift(grads[step], "x", 4, step) for step in (1, 3, 2)]
    result = backward(
        (back, back_rest), (weight, weight_rest), inputs, scale_inv, norm_gain[None], incoming
    )
    result, *along_x = join(result, *along_x)

    rows = channels // 16
    by_y = []
    for step in range(4):
        start = ((y + step) % 4) * rows
        parts = [lax.dynamic_slice_in_dim(part, start, rows, axis=1) for part in along_x]
        by_y.append(sum(part.astype(F32) for part in parts))
    total = by_y[0]
    for step in (1, 3, 2):
        total = total + shift(by_y[step].astype(BF16), RING_Y, 4, step).astype(F32)
    weight_grad = share_weight_grad(total, yl, core)
    total_rows = 16 * 16 * count
    return (result[None], weight_grad / math.sqrt(total_rows))


def solution(mesh):
    grid = Mesh(mesh.devices.reshape(SIZES), AXES)
    dp, seq = ("x", "yh", "core"), SEQ
    in_specs = (
        P(dp, seq, None),
        P(dp, seq),
        P(),
        P(),
        P(None, dp, None),
        P(dp, seq, None),
    )
    out_specs = (P(dp, seq, None), P(None, dp, None))
    return jax.shard_map(
        on_device, mesh=grid, in_specs=in_specs, out_specs=out_specs, check_vma=False
    )
```

```python
import functools
import math

import jax
import jax.numpy as jnp
from jax import lax
from jax.experimental import pallas as pl
from jax.experimental.pallas import tpu as pltpu
from jax.sharding import Mesh, PartitionSpec as P

FILTER_TAPS = 3
DILATION_STEP = 32
REACH = 32
AXES = ("x", "yh", "core", "yl", "z")
SIZES = (4, 2, 2, 2, 8)
SEQ = ("yl", "z")
RING_Y = ("yh", "yl")
BF16 = jnp.bfloat16
F32 = jnp.float32


def shift(value, axis, count, step):
    pairs = [(i, (i + step) % count) for i in range(count)]
    return lax.ppermute(value, axis, pairs)


def swap(value, axis, count, mask):
    return lax.ppermute(value, axis, [(i, i ^ mask) for i in range(count)])


def gelu_slope(value):
    coeff = math.sqrt(2.0 / math.pi)
    square = value * value
    tangent = jnp.tanh(value * (coeff + coeff * 0.044715 * square))
    return (0.5 + 0.5 * tangent) * (
        1.0 + value * (1.0 - tangent) * (coeff + coeff * 3.0 * 0.044715 * square)
    )


def join(*arrays):
    return lax.optimization_barrier(arrays)


def load_weight(position, pieces, weight, sem):
    x, yh, core = position[0], position[1], position[2]
    rows = pieces[0].shape[2]
    steps = [(0, 0), (0, 1), (3, 0), (3, 1), (1, 0), (1, 1), (2, 0), (2, 1)]
    copies = []
    for block, (step_x, step_y) in zip(pieces, steps):
        for side in range(2):
            owner = ((x + step_x) % 4) * 4 + ((yh + step_y) % 2) * 2 + (core + side) % 2
            place = pl.multiple_of(owner * rows, 16)
            copies.append(
                pltpu.make_async_copy(
                    block.at[side], weight.at[:, pl.ds(place, rows), :], sem.at[len(copies)]
                )
            )
    return copies


def forward_kernel(position, *refs):
    pieces, refs = refs[:8], refs[8:]
    normed_hbm, edges, upstream_hbm = refs[0:2], refs[2:4], refs[4:6]
    weight_out, back_out, grad_out = refs[6], refs[7:9], refs[9]
    weight, normed, upstream, back, grad = refs[10:15]
    piece_sem, load_sem, back_sem, weight_sem, grad_sem = refs[15:]
    core = position[2]
    channels, half = weight.shape[1:]
    count = normed_hbm[0].shape[0]
    lane = pl.multiple_of(core * half, 128)
    copies = load_weight(position, pieces, weight, piece_sem)
    wide = 2 * REACH
    loads = []
    for index in range(2):
        center = upstream_hbm[index]
        if index == 0:
            center = center.at[:, pl.ds(lane, half)]
        rows, lanes = slice(index * wide, (index + 1) * wide), slice(index * half, (index + 1) * half)
        moves = [
            (normed_hbm[index], normed.at[index, wide : wide + count]),
            (center, upstream.at[index, REACH : REACH + count]),
        ]
        for edge, place in zip(edges, (0, wide + count)):
            moves.append((edge.at[rows], normed.at[index, place : place + wide]))
        for edge, place in zip(edges, (0, REACH + count)):
            moves.append((edge.at[2 * wide :, lanes], upstream.at[index, place : place + REACH]))
        loads.append(
            [
                pltpu.make_async_copy(source, target, load_sem.at[index, place])
                for place, (source, target) in enumerate(moves)
            ]
        )
    for copy in copies + loads[0] + loads[1]:
        copy.start()
    for copy in copies:
        copy.wait()
    save = pltpu.make_async_copy(weight, weight_out, weight_sem)
    save.start()
    length = back.shape[1]
    block = length // 3
    saves = [save]
    for index in range(2):
        for copy in loads[index]:
            copy.wait()
        for start in range(0, length, block):
            conv = jnp.dot(
                normed[index, start : start + block, :], weight[0], preferred_element_type=F32
            )
            for tap in range(1, FILTER_TAPS):
                low = start + tap * DILATION_STEP
                conv = conv + jnp.dot(
                    normed[index, low : low + block, :], weight[tap], preferred_element_type=F32
                )
            incoming = upstream[index, start : start + block, :].astype(F32)
            back[index, start : start + block, :] = (incoming * gelu_slope(conv)).astype(BF16)
        back_save = pltpu.make_async_copy(back.at[index], back_out[index], back_sem.at[index])
        back_save.start()
        saves.append(back_save)
    total = None
    for index in range(2):
        shifted = jnp.concatenate(
            [
                back[index, wide - tap * DILATION_STEP : wide - tap * DILATION_STEP + count, :]
                for tap in range(FILTER_TAPS)
            ],
            axis=1,
        )
        part = lax.dot_general(
            normed[index, wide : wide + count, :],
            shifted,
            (((0,), (0,)), ((), ())),
            preferred_element_type=F32,
        )
        total = part if total is None else total + part
    for tap in range(FILTER_TAPS):
        grad[tap] = total[:, tap * half : (tap + 1) * half].astype(BF16)
    owners, _, rows, _ = grad_out.shape
    for owner in range(owners):
        grad_save = pltpu.make_async_copy(
            grad.at[:, owner * rows : (owner + 1) * rows, :],
            grad_out.at[owner],
            grad_sem.at[owner],
        )
        grad_save.start()
        saves.append(grad_save)
    for copy in saves:
        copy.wait()


def forward(position, pieces, normed, edges, upstream):
    count, channels = normed[0].shape
    half = channels // 2
    length = count + 2 * REACH
    anywhere = pl.BlockSpec(memory_space=pl.ANY)
    dma = pltpu.SemaphoreType.DMA
    return pl.pallas_call(
        forward_kernel,
        out_shape=[jax.ShapeDtypeStruct((FILTER_TAPS, channels, half), BF16)]
        + [jax.ShapeDtypeStruct((length, half), BF16)] * 2
        + [jax.ShapeDtypeStruct((16, FILTER_TAPS, channels // 16, half), BF16)],
        in_specs=[pl.BlockSpec(memory_space=pltpu.SMEM)] + [anywhere] * 14,
        out_specs=[anywhere] * 4,
        scratch_shapes=[
            pltpu.VMEM((FILTER_TAPS, channels, half), BF16),
            pltpu.VMEM((2, length + 2 * REACH, channels), BF16),
            pltpu.VMEM((2, length, half), BF16),
            pltpu.VMEM((2, length, half), BF16),
            pltpu.VMEM((FILTER_TAPS, channels, half), BF16),
            dma((16,)),
            dma((2, 6)),
            dma((2,)),
            dma,
            dma((16,)),
        ],
        compiler_params=pltpu.CompilerParams(vmem_limit_bytes=56 * 1024 * 1024),
        name="forward",
    )(position, *pieces, *normed, *edges, *upstream)


def backward_kernel(back_a, back_b, weight_a, weight_b, inputs, scale, gain, incoming, out):
    block = out.shape[0]
    start = pl.program_id(0) * block
    grad = jnp.zeros(out.shape, F32)
    for tap in range(FILTER_TAPS):
        low = pl.multiple_of(start + (FILTER_TAPS - 1 - tap) * DILATION_STEP, 32)
        rows = pl.ds(low, block)
        grad = grad + lax.dot_general(
            jnp.concatenate([back_a[rows, :], back_b[rows, :]], axis=1),
            jnp.concatenate([weight_a[tap], weight_b[tap]], axis=1),
            (((1,), (1,)), ((), ())),
            preferred_element_type=F32,
        )
    scaled = grad * gain[...]
    value = inputs[...]
    factor = scale[...]
    spread = jnp.mean(scaled * value, axis=-1, keepdims=True)
    result = incoming[...].astype(F32) + factor * scaled - value * (factor * factor * factor * spread)
    out[...] = result.astype(BF16)


def backward(back, weight, inputs, scale, gain, incoming):
    count, channels = inputs.shape
    block = 256
    whole = lambda array: pl.BlockSpec(array.shape, lambda i: (0,) * array.ndim)
    part = pl.BlockSpec((block, channels), lambda i: (i, 0))
    return pl.pallas_call(
        backward_kernel,
        grid=(count // block,),
        out_shape=jax.ShapeDtypeStruct((count, channels), BF16),
        in_specs=[whole(back[0]), whole(back[1]), whole(weight[0]), whole(weight[1]), part]
        + [pl.BlockSpec((block, 1), lambda i: (i, 0)), whole(gain), part],
        out_specs=part,
        compiler_params=pltpu.CompilerParams(vmem_limit_bytes=56 * 1024 * 1024),
        name="backward",
    )(*back, *weight, inputs, scale, gain, incoming)


def share_weight_grad(total, yl, core):
    sent = total.astype(BF16)
    near, middle, far = (swap(sent, "z", 8, mask).astype(F32) for mask in (1, 2, 3))
    sent = ((sent.astype(F32) + near) + (middle + far)).astype(BF16)
    mine = (sent.astype(F32) + swap(sent, "z", 8, 7).astype(F32)).astype(BF16)
    pair = ("core", "yl")
    first = lax.ppermute(mine, pair, [(2, 0), (1, 3), (0, 1), (3, 2)])
    second = lax.ppermute(mine, pair, [(2, 1), (1, 2)])
    here = jnp.where(core == yl, mine, first)
    there = jnp.where(core == yl, first, second)
    low = jnp.where(core == 0, here, there)
    high = jnp.where(core == 0, there, here)
    return jnp.concatenate([low, high], axis=2).astype(F32)


def on_device(activations, nucleotides, base_table, norm_gain, filter_weight, upstream):
    x, yh, core, yl = (lax.axis_index(name) for name in ("x", "yh", "core", "yl"))
    position = jnp.stack([x, yh, core, yl]).astype(jnp.int32)
    tokens, incoming = activations[0], upstream[0]
    count, channels = tokens.shape
    half = channels // 2

    mine = lax.dynamic_slice_in_dim(filter_weight, core * half, half, axis=2)
    other = lax.dynamic_slice_in_dim(filter_weight, (1 - core) * half, half, axis=2)
    own = jnp.stack([mine, swap(other, "core", 2, 1)])
    own, tokens, nucleotides, incoming = join(own, tokens, nucleotides, incoming)

    across = swap(own, RING_Y, 4, 3)
    around_own = [shift(own, "x", 4, step) for step in (1, -1, 2)]
    bases = nucleotides[0][:, None]
    row = base_table[3][None]
    for base in (2, 1, 0):
        row = jnp.where(bases == base, base_table[base][None], row)
    inputs = tokens.astype(F32) + row
    square = jnp.mean(inputs * inputs, axis=-1)
    across, inputs, square, incoming, *around_own = join(
        across, inputs, square, incoming, *around_own
    )

    around_across = [shift(across, "x", 4, step) for step in (1, -1, 2)]
    scale_inv = lax.rsqrt(square + 1e-06)[:, None]
    normed = (inputs * scale_inv * norm_gain).astype(BF16)
    upstream_sent = lax.dynamic_slice_in_dim(incoming, (1 - core) * half, half, axis=1)
    normed_other = swap(normed, "core", 2, 1)
    upstream_other = swap(upstream_sent, "core", 2, 1)
    around_across[0], around_across[1], normed, normed_other, upstream_other, incoming = join(
        around_across[0], around_across[1], normed, normed_other, upstream_other, incoming
    )

    def edge(rows, reach_rows):
        upstream_edge = lax.dynamic_slice_in_dim(incoming[reach_rows], core * half, half, axis=1)
        upstream_edge = jnp.concatenate([upstream_edge, upstream_other[reach_rows]], axis=1)
        return jnp.concatenate([normed[rows], normed_other[rows], upstream_edge])

    low = lax.ppermute(
        edge(slice(count - 2 * REACH, count), slice(count - REACH, count)),
        SEQ,
        [(i, i + 1) for i in range(15)],
    )
    high = lax.ppermute(
        edge(slice(0, 2 * REACH), slice(0, REACH)), SEQ, [(i + 1, i) for i in range(15)]
    )
    pieces = [own, across]
    for pair in zip(around_own, around_across):
        pieces += pair
    weight, back, back_other, grads = forward(
        position,
        pieces,
        (normed, normed_other),
        (low, high),
        (incoming, upstream_other),
    )

    back_rest = swap(back_other, "core", 2, 1)
    weight_rest = swap(weight, "core", 2, 1)
    arrived = lax.all_to_all(grads, ("x", "yh", "yl"), 0, 0, tiled=True)
    result = backward(
        (back, back_rest), (weight, weight_rest), inputs, scale_inv, norm_gain[None], incoming
    )
    result, arrived = join(result, arrived)
    total = jnp.sum(arrived.astype(F32), axis=0)
    weight_grad = share_weight_grad(total, yl, core)
    total_rows = 16 * 16 * count
    return (result[None], weight_grad / math.sqrt(total_rows))


def solution(mesh):
    grid = Mesh(mesh.devices.reshape(SIZES), AXES)
    dp, seq = ("x", "yh", "core"), SEQ
    in_specs = (
        P(dp, seq, None),
        P(dp, seq),
        P(),
        P(),
        P(None, dp, None),
        P(dp, seq, None),
    )
    out_specs = (P(dp, seq, None), P(None, dp, None))
    return jax.shard_map(
        on_device, mesh=grid, in_specs=in_specs, out_specs=out_specs, check_vma=False
    )
```

```python
import functools
import math

import jax
import jax.numpy as jnp
from jax import lax
from jax.experimental import pallas as pl
from jax.experimental.pallas import tpu as pltpu
from jax.sharding import Mesh, PartitionSpec as P

FILTER_TAPS = 3
DILATION_STEP = 32
REACH = 32
AXES = ("x", "yh", "core", "yl", "z")
SIZES = (4, 2, 2, 2, 8)
SEQ = ("yl", "z")
RING_Y = ("yh", "yl")
BF16 = jnp.bfloat16
F32 = jnp.float32


def shift(value, axis, count, step):
    pairs = [(i, (i + step) % count) for i in range(count)]
    return lax.ppermute(value, axis, pairs)


def swap(value, axis, count, mask):
    return lax.ppermute(value, axis, [(i, i ^ mask) for i in range(count)])


def gelu_slope(value):
    coeff = math.sqrt(2.0 / math.pi)
    square = value * value
    tangent = jnp.tanh(value * (coeff + coeff * 0.044715 * square))
    return (0.5 + 0.5 * tangent) * (
        1.0 + value * (1.0 - tangent) * (coeff + coeff * 3.0 * 0.044715 * square)
    )


def join(*arrays):
    return lax.optimization_barrier(arrays)


def load_weight(position, pieces, weight, sem):
    x, yh, core = position[0], position[1], position[2]
    rows = pieces[0].shape[2]
    steps = [(0, 0), (0, 1), (3, 0), (3, 1), (1, 0), (1, 1), (2, 0), (2, 1)]
    blocks = list(pieces[:6]) + [pieces[6].at[0], pieces[6].at[1]]
    copies = []
    for block, (step_x, step_y) in zip(blocks, steps):
        for side in range(2):
            owner = ((x + step_x) % 4) * 4 + ((yh + step_y) % 2) * 2 + (core + side) % 2
            place = pl.multiple_of(owner * rows, 16)
            copies.append(
                pltpu.make_async_copy(
                    block.at[side], weight.at[:, pl.ds(place, rows), :], sem.at[len(copies)]
                )
            )
    return copies


def forward_kernel(position, *refs):
    pieces, refs = refs[:7], refs[7:]
    normed_hbm, edges, upstream_hbm = refs[0:2], refs[2:4], refs[4:6]
    weight_out, back_out, grad_out = refs[6], refs[7:9], refs[9]
    weight, normed, upstream, back, grad = refs[10:15]
    piece_sem, load_sem, back_sem, weight_sem, grad_sem = refs[15:]
    core = position[2]
    channels, half = weight.shape[1:]
    count = normed_hbm[0].shape[0]
    lane = pl.multiple_of(core * half, 128)
    copies = load_weight(position, pieces, weight, piece_sem)
    wide = 2 * REACH
    loads = []
    for index in range(2):
        center = upstream_hbm[index]
        if index == 0:
            center = center.at[:, pl.ds(lane, half)]
        rows, lanes = pl.ds(index * wide, wide), pl.ds(index * half, half)
        moves = [
            (normed_hbm[index], normed.at[index, wide : wide + count]),
            (center, upstream.at[index, REACH : REACH + count]),
            (edges[0].at[rows], normed.at[index, :wide]),
            (edges[1].at[rows], normed.at[index, wide + count :]),
            (edges[0].at[2 * wide :, lanes], upstream.at[index, :REACH]),
            (edges[1].at[2 * wide :, lanes], upstream.at[index, REACH + count :]),
        ]
        loads.append(
            [
                pltpu.make_async_copy(source, target, load_sem.at[index, place])
                for place, (source, target) in enumerate(moves)
            ]
        )
    for copy in copies + loads[0] + loads[1]:
        copy.start()
    for copy in copies:
        copy.wait()
    save = pltpu.make_async_copy(weight, weight_out, weight_sem)
    save.start()
    length = back.shape[1]
    block = length // 3
    saves = [save]
    for index in range(2):
        for copy in loads[index]:
            copy.wait()
        for start in range(0, length, block):
            conv = jnp.dot(
                normed[index, start : start + block, :], weight[0], preferred_element_type=F32
            )
            for tap in range(1, FILTER_TAPS):
                low = start + tap * DILATION_STEP
                conv = conv + jnp.dot(
                    normed[index, low : low + block, :], weight[tap], preferred_element_type=F32
                )
            incoming = upstream[index, start : start + block, :].astype(F32)
            back[index, start : start + block, :] = (incoming * gelu_slope(conv)).astype(BF16)
        back_save = pltpu.make_async_copy(back.at[index], back_out[index], back_sem.at[index])
        back_save.start()
        saves.append(back_save)
    total = None
    for index in range(2):
        shifted = jnp.concatenate(
            [
                back[index, wide - tap * DILATION_STEP : wide - tap * DILATION_STEP + count, :]
                for tap in range(FILTER_TAPS)
            ],
            axis=1,
        )
        part = lax.dot_general(
            normed[index, wide : wide + count, :],
            shifted,
            (((0,), (0,)), ((), ())),
            preferred_element_type=F32,
        )
        total = part if total is None else total + part
    for tap in range(FILTER_TAPS):
        grad[tap] = total[:, tap * half : (tap + 1) * half].astype(BF16)
    owners, _, rows, _ = grad_out.shape
    for owner in range(owners):
        grad_save = pltpu.make_async_copy(
            grad.at[:, owner * rows : (owner + 1) * rows, :],
            grad_out.at[owner],
            grad_sem.at[owner],
        )
        grad_save.start()
        saves.append(grad_save)
    for copy in saves:
        copy.wait()


def forward(position, pieces, normed, edges, upstream):
    count, channels = normed[0].shape
    half = channels // 2
    length = count + 2 * REACH
    anywhere = pl.BlockSpec(memory_space=pl.ANY)
    dma = pltpu.SemaphoreType.DMA
    return pl.pallas_call(
        forward_kernel,
        out_shape=[jax.ShapeDtypeStruct((FILTER_TAPS, channels, half), BF16)]
        + [jax.ShapeDtypeStruct((length, half), BF16)] * 2
        + [jax.ShapeDtypeStruct((16, FILTER_TAPS, channels // 16, half), BF16)],
        in_specs=[pl.BlockSpec(memory_space=pltpu.SMEM)] + [anywhere] * 13,
        out_specs=[anywhere] * 4,
        scratch_shapes=[
            pltpu.VMEM((FILTER_TAPS, channels, half), BF16),
            pltpu.VMEM((2, length + 2 * REACH, channels), BF16),
            pltpu.VMEM((2, length, half), BF16),
            pltpu.VMEM((2, length, half), BF16),
            pltpu.VMEM((FILTER_TAPS, channels, half), BF16),
            dma((16,)),
            dma((2, 6)),
            dma((2,)),
            dma,
            dma((16,)),
        ],
        compiler_params=pltpu.CompilerParams(vmem_limit_bytes=26 * 1024 * 1024),
        name="forward",
    )(position, *pieces, *normed, *edges, *upstream)


def backward_kernel(back_a, back_b, weight_a, weight_b, inputs, scale, gain, incoming, out):
    block = out.shape[0]
    start = pl.program_id(0) * block
    grad = jnp.zeros(out.shape, F32)
    for tap in range(FILTER_TAPS):
        low = pl.multiple_of(start + (FILTER_TAPS - 1 - tap) * DILATION_STEP, 32)
        rows = pl.ds(low, block)
        grad = grad + lax.dot_general(
            jnp.concatenate([back_a[rows, :], back_b[rows, :]], axis=1),
            jnp.concatenate([weight_a[tap], weight_b[tap]], axis=1),
            (((1,), (1,)), ((), ())),
            preferred_element_type=F32,
        )
    scaled = grad * gain[...]
    value = inputs[...]
    factor = scale[...]
    spread = jnp.mean(scaled * value, axis=-1, keepdims=True)
    result = incoming[...].astype(F32) + factor * scaled - value * (factor * factor * factor * spread)
    out[...] = result.astype(BF16)


def backward(back, weight, inputs, scale, gain, incoming):
    count, channels = inputs.shape
    block = 256
    whole = lambda array: pl.BlockSpec(array.shape, lambda i: (0,) * array.ndim)
    part = pl.BlockSpec((block, channels), lambda i: (i, 0))
    return pl.pallas_call(
        backward_kernel,
        grid=(count // block,),
        out_shape=jax.ShapeDtypeStruct((count, channels), BF16),
        in_specs=[whole(back[0]), whole(back[1]), whole(weight[0]), whole(weight[1]), part]
        + [pl.BlockSpec((block, 1), lambda i: (i, 0)), whole(gain), part],
        out_specs=part,
        compiler_params=pltpu.CompilerParams(vmem_limit_bytes=26 * 1024 * 1024),
        name="backward",
    )(*back, *weight, inputs, scale, gain, incoming)


def share_weight_grad(total, yl, core):
    sent = total.astype(BF16)
    near, middle, far = (swap(sent, "z", 8, mask).astype(F32) for mask in (1, 2, 3))
    sent = ((sent.astype(F32) + near) + (middle + far)).astype(BF16)
    mine = (sent.astype(F32) + swap(sent, "z", 8, 7).astype(F32)).astype(BF16)
    pair = ("core", "yl")
    first = lax.ppermute(mine, pair, [(2, 0), (1, 3), (0, 1), (3, 2)])
    second = lax.ppermute(mine, pair, [(2, 1), (1, 2)])
    here = jnp.where(core == yl, mine, first)
    there = jnp.where(core == yl, first, second)
    low = jnp.where(core == 0, here, there)
    high = jnp.where(core == 0, there, here)
    return jnp.concatenate([low, high], axis=2).astype(F32)


def on_device(activations, nucleotides, base_table, norm_gain, filter_weight, upstream):
    x, yh, core, yl = (lax.axis_index(name) for name in ("x", "yh", "core", "yl"))
    position = jnp.stack([x, yh, core, yl]).astype(jnp.int32)
    tokens, incoming = activations[0], upstream[0]
    count, channels = tokens.shape
    half = channels // 2

    mine = lax.dynamic_slice_in_dim(filter_weight, core * half, half, axis=2)
    other = lax.dynamic_slice_in_dim(filter_weight, (1 - core) * half, half, axis=2)
    own = jnp.stack([mine, swap(other, "core", 2, 1)])
    own, tokens, nucleotides, incoming = join(own, tokens, nucleotides, incoming)

    across = swap(own, RING_Y, 4, 3)
    up_own, down_own = shift(own, "x", 4, 1), shift(own, "x", 4, -1)
    bases = nucleotides[0][:, None]
    row = base_table[3][None]
    for base in (2, 1, 0):
        row = jnp.where(bases == base, base_table[base][None], row)
    inputs = tokens.astype(F32) + row
    scale_inv = lax.rsqrt(jnp.mean(inputs * inputs, axis=-1, keepdims=True) + 1e-06)
    normed = (inputs * scale_inv * norm_gain).astype(BF16)
    own, across, up_own, down_own, normed, incoming = join(
        own, across, up_own, down_own, normed, incoming
    )

    far = shift(jnp.stack([own, across]), "x", 4, 2)
    up_across, down_across = shift(across, "x", 4, 1), shift(across, "x", 4, -1)
    upstream_sent = lax.dynamic_slice_in_dim(incoming, (1 - core) * half, half, axis=1)
    normed_other = swap(normed, "core", 2, 1)
    upstream_other = swap(upstream_sent, "core", 2, 1)

    def edge(rows, reach_rows):
        upstream_edge = lax.dynamic_slice_in_dim(incoming[reach_rows], core * half, half, axis=1)
        upstream_edge = jnp.concatenate([upstream_edge, upstream_other[reach_rows]], axis=1)
        return jnp.concatenate([normed[rows], normed_other[rows], upstream_edge])

    last = edge(slice(count - 2 * REACH, count), slice(count - REACH, count))
    first = edge(slice(0, 2 * REACH), slice(0, REACH))
    edges = (
        lax.ppermute(last, SEQ, [(i, i + 1) for i in range(15)]),
        lax.ppermute(first, SEQ, [(i + 1, i) for i in range(15)]),
    )
    weight, back, back_other, grads = forward(
        position,
        [own, across, up_own, up_across, down_own, down_across, far],
        (normed, normed_other),
        edges,
        (incoming, upstream_other),
    )

    back_rest = swap(back_other, "core", 2, 1)
    weight_rest = swap(weight, "core", 2, 1)
    arrived = lax.all_to_all(grads, ("x", "yh", "yl"), 0, 0, tiled=True)
    result = backward(
        (back, back_rest), (weight, weight_rest), inputs, scale_inv, norm_gain[None], incoming
    )
    result, arrived = join(result, arrived)
    total = jnp.sum(arrived.astype(F32), axis=0)
    weight_grad = share_weight_grad(total, yl, core)
    total_rows = 16 * 16 * count
    return (result[None], weight_grad / math.sqrt(total_rows))


def solution(mesh):
    grid = Mesh(mesh.devices.reshape(SIZES), AXES)
    dp, seq = ("x", "yh", "core"), SEQ
    in_specs = (
        P(dp, seq, None),
        P(dp, seq),
        P(),
        P(),
        P(None, dp, None),
        P(dp, seq, None),
    )
    out_specs = (P(dp, seq, None), P(None, dp, None))
    return jax.shard_map(
        on_device, mesh=grid, in_specs=in_specs, out_specs=out_specs, check_vma=False
    )
```

```python
import functools
import math

import jax
import jax.numpy as jnp
from jax import lax
from jax.experimental import pallas as pl
from jax.experimental.pallas import tpu as pltpu
from jax.sharding import Mesh, PartitionSpec as P

FILTER_TAPS = 3
DILATION_STEP = 32
REACH = 32
AXES = ("x", "yh", "core", "yl", "z")
SIZES = (4, 2, 2, 2, 8)
SEQ = ("yl", "z")
RING_Y = ("yh", "yl")
BF16 = jnp.bfloat16
F32 = jnp.float32


def shift(value, axis, count, step):
    pairs = [(i, (i + step) % count) for i in range(count)]
    return lax.ppermute(value, axis, pairs)


def swap(value, axis, count, mask):
    return lax.ppermute(value, axis, [(i, i ^ mask) for i in range(count)])


def gelu_slope(value):
    coeff = math.sqrt(2.0 / math.pi)
    square = value * value
    tangent = jnp.tanh(value * (coeff + coeff * 0.044715 * square))
    return (0.5 + 0.5 * tangent) * (
        1.0 + value * (1.0 - tangent) * (coeff + coeff * 3.0 * 0.044715 * square)
    )


def join(*arrays):
    return lax.optimization_barrier(arrays)


def load_weight(position, pieces, weight, sem):
    x, yh, core = position[0], position[1], position[2]
    rows = pieces[0].shape[2]
    steps = [(0, 0), (0, 1), (3, 0), (3, 1), (1, 0), (1, 1), (2, 0), (2, 1)]
    blocks = list(pieces[:6]) + [pieces[6].at[0], pieces[6].at[1]]
    copies = []
    for block, (step_x, step_y) in zip(blocks, steps):
        for side in range(2):
            owner = ((x + step_x) % 4) * 4 + ((yh + step_y) % 2) * 2 + (core + side) % 2
            place = pl.multiple_of(owner * rows, 16)
            copies.append(
                pltpu.make_async_copy(
                    block.at[side], weight.at[:, pl.ds(place, rows), :], sem.at[len(copies)]
                )
            )
    return copies


def forward_kernel(position, *refs):
    pieces, refs = refs[:7], refs[7:]
    normed_hbm, edges, upstream_hbm = refs[0:2], refs[2:4], refs[4:6]
    weight_out, back_out, grad_out = refs[6], refs[7:9], refs[9:13]
    weight, normed, upstream, back, grad = refs[13:18]
    piece_sem, load_sem, back_sem, weight_sem, grad_sem = refs[18:]
    x, core = position[0], position[2]
    channels, half = weight.shape[1:]
    count = normed_hbm[0].shape[0]
    lane = pl.multiple_of(core * half, 128)
    copies = load_weight(position, pieces, weight, piece_sem)
    wide = 2 * REACH
    loads = []
    for index in range(2):
        center = upstream_hbm[index]
        if index == 0:
            center = center.at[:, pl.ds(lane, half)]
        rows, lanes = pl.ds(index * wide, wide), pl.ds(index * half, half)
        moves = [
            (normed_hbm[index], normed.at[index, wide : wide + count]),
            (center, upstream.at[index, REACH : REACH + count]),
            (edges[0].at[rows], normed.at[index, :wide]),
            (edges[1].at[rows], normed.at[index, wide + count :]),
            (edges[0].at[2 * wide :, lanes], upstream.at[index, :REACH]),
            (edges[1].at[2 * wide :, lanes], upstream.at[index, REACH + count :]),
        ]
        loads.append(
            [
                pltpu.make_async_copy(source, target, load_sem.at[index, place])
                for place, (source, target) in enumerate(moves)
            ]
        )
    for copy in copies + loads[0] + loads[1]:
        copy.start()
    for copy in copies:
        copy.wait()
    save = pltpu.make_async_copy(weight, weight_out, weight_sem)
    save.start()
    length = back.shape[1]
    block = length // 3
    saves = [save]
    for index in range(2):
        for copy in loads[index]:
            copy.wait()
        for start in range(0, length, block):
            conv = jnp.dot(
                normed[index, start : start + block, :], weight[0], preferred_element_type=F32
            )
            for tap in range(1, FILTER_TAPS):
                low = start + tap * DILATION_STEP
                conv = conv + jnp.dot(
                    normed[index, low : low + block, :], weight[tap], preferred_element_type=F32
                )
            incoming = upstream[index, start : start + block, :].astype(F32)
            back[index, start : start + block, :] = (incoming * gelu_slope(conv)).astype(BF16)
        back_save = pltpu.make_async_copy(back.at[index], back_out[index], back_sem.at[index])
        back_save.start()
        saves.append(back_save)
    total = None
    for index in range(2):
        shifted = jnp.concatenate(
            [
                back[index, wide - tap * DILATION_STEP : wide - tap * DILATION_STEP + count, :]
                for tap in range(FILTER_TAPS)
            ],
            axis=1,
        )
        part = lax.dot_general(
            normed[index, wide : wide + count, :],
            shifted,
            (((0,), (0,)), ((), ())),
            preferred_element_type=F32,
        )
        total = part if total is None else total + part
    for tap in range(FILTER_TAPS):
        grad[tap] = total[:, tap * half : (tap + 1) * half].astype(BF16)
    quarter = channels // 4
    for step in range(4):
        place = pl.multiple_of(((x + step) % 4) * quarter, 16)
        grad_save = pltpu.make_async_copy(
            grad.at[:, pl.ds(place, quarter), :], grad_out[step], grad_sem.at[step]
        )
        grad_save.start()
        saves.append(grad_save)
    for copy in saves:
        copy.wait()


def forward(position, pieces, normed, edges, upstream):
    count, channels = normed[0].shape
    half = channels // 2
    length = count + 2 * REACH
    anywhere = pl.BlockSpec(memory_space=pl.ANY)
    dma = pltpu.SemaphoreType.DMA
    return pl.pallas_call(
        forward_kernel,
        out_shape=[jax.ShapeDtypeStruct((FILTER_TAPS, channels, half), BF16)]
        + [jax.ShapeDtypeStruct((length, half), BF16)] * 2
        + [jax.ShapeDtypeStruct((FILTER_TAPS, channels // 4, half), BF16)] * 4,
        in_specs=[pl.BlockSpec(memory_space=pltpu.SMEM)] + [anywhere] * 13,
        out_specs=[anywhere] * 7,
        scratch_shapes=[
            pltpu.VMEM((FILTER_TAPS, channels, half), BF16),
            pltpu.VMEM((2, length + 2 * REACH, channels), BF16),
            pltpu.VMEM((2, length, half), BF16),
            pltpu.VMEM((2, length, half), BF16),
            pltpu.VMEM((FILTER_TAPS, channels, half), BF16),
            dma((16,)),
            dma((2, 6)),
            dma((2,)),
            dma,
            dma((4,)),
        ],
        compiler_params=pltpu.CompilerParams(vmem_limit_bytes=26 * 1024 * 1024),
        name="forward",
    )(position, *pieces, *normed, *edges, *upstream)


def backward_kernel(back_a, back_b, weight_a, weight_b, inputs, scale, gain, incoming, out):
    block = out.shape[0]
    start = pl.program_id(0) * block
    grad = jnp.zeros(out.shape, F32)
    for tap in range(FILTER_TAPS):
        low = pl.multiple_of(start + (FILTER_TAPS - 1 - tap) * DILATION_STEP, 32)
        rows = pl.ds(low, block)
        grad = grad + lax.dot_general(
            jnp.concatenate([back_a[rows, :], back_b[rows, :]], axis=1),
            jnp.concatenate([weight_a[tap], weight_b[tap]], axis=1),
            (((1,), (1,)), ((), ())),
            preferred_element_type=F32,
        )
    scaled = grad * gain[...]
    value = inputs[...]
    factor = scale[...]
    spread = jnp.mean(scaled * value, axis=-1, keepdims=True)
    result = incoming[...].astype(F32) + factor * scaled - value * (factor * factor * factor * spread)
    out[...] = result.astype(BF16)


def backward(back, weight, inputs, scale, gain, incoming):
    count, channels = inputs.shape
    block = 256
    whole = lambda array: pl.BlockSpec(array.shape, lambda i: (0,) * array.ndim)
    part = pl.BlockSpec((block, channels), lambda i: (i, 0))
    return pl.pallas_call(
        backward_kernel,
        grid=(count // block,),
        out_shape=jax.ShapeDtypeStruct((count, channels), BF16),
        in_specs=[whole(back[0]), whole(back[1]), whole(weight[0]), whole(weight[1]), part]
        + [pl.BlockSpec((block, 1), lambda i: (i, 0)), whole(gain), part],
        out_specs=part,
        compiler_params=pltpu.CompilerParams(vmem_limit_bytes=26 * 1024 * 1024),
        name="backward",
    )(*back, *weight, inputs, scale, gain, incoming)


def share_weight_grad(total, yl, core):
    sent = total.astype(BF16)
    near, middle, far = (swap(sent, "z", 8, mask).astype(F32) for mask in (1, 2, 3))
    sent = ((sent.astype(F32) + near) + (middle + far)).astype(BF16)
    mine = (sent.astype(F32) + swap(sent, "z", 8, 7).astype(F32)).astype(BF16)
    pair = ("core", "yl")
    first = lax.ppermute(mine, pair, [(2, 0), (1, 3), (0, 1), (3, 2)])
    second = lax.ppermute(mine, pair, [(2, 1), (1, 2)])
    here = jnp.where(core == yl, mine, first)
    there = jnp.where(core == yl, first, second)
    low = jnp.where(core == 0, here, there)
    high = jnp.where(core == 0, there, here)
    return jnp.concatenate([low, high], axis=2).astype(F32)


def on_device(activations, nucleotides, base_table, norm_gain, filter_weight, upstream):
    x, yh, core, yl = (lax.axis_index(name) for name in ("x", "yh", "core", "yl"))
    y = yh * 2 + yl
    position = jnp.stack([x, yh, core, yl]).astype(jnp.int32)
    tokens, incoming = activations[0], upstream[0]
    count, channels = tokens.shape
    half = channels // 2

    mine = lax.dynamic_slice_in_dim(filter_weight, core * half, half, axis=2)
    other = lax.dynamic_slice_in_dim(filter_weight, (1 - core) * half, half, axis=2)
    own = jnp.stack([mine, swap(other, "core", 2, 1)])
    own, tokens, nucleotides, incoming = join(own, tokens, nucleotides, incoming)

    across = swap(own, RING_Y, 4, 3)
    up_own, down_own = shift(own, "x", 4, 1), shift(own, "x", 4, -1)
    bases = nucleotides[0][:, None]
    row = base_table[3][None]
    for base in (2, 1, 0):
        row = jnp.where(bases == base, base_table[base][None], row)
    inputs = tokens.astype(F32) + row
    scale_inv = lax.rsqrt(jnp.mean(inputs * inputs, axis=-1, keepdims=True) + 1e-06)
    normed = (inputs * scale_inv * norm_gain).astype(BF16)
    own, across, up_own, down_own, normed, incoming = join(
        own, across, up_own, down_own, normed, incoming
    )

    far = shift(jnp.stack([own, across]), "x", 4, 2)
    up_across, down_across = shift(across, "x", 4, 1), shift(across, "x", 4, -1)
    upstream_sent = lax.dynamic_slice_in_dim(incoming, (1 - core) * half, half, axis=1)
    normed_other = swap(normed, "core", 2, 1)
    upstream_other = swap(upstream_sent, "core", 2, 1)

    def edge(rows, reach_rows):
        upstream_edge = lax.dynamic_slice_in_dim(incoming[reach_rows], core * half, half, axis=1)
        upstream_edge = jnp.concatenate([upstream_edge, upstream_other[reach_rows]], axis=1)
        return jnp.concatenate([normed[rows], normed_other[rows], upstream_edge])

    last = edge(slice(count - 2 * REACH, count), slice(count - REACH, count))
    first = edge(slice(0, 2 * REACH), slice(0, REACH))
    edges = (
        lax.ppermute(last, SEQ, [(i, i + 1) for i in range(15)]),
        lax.ppermute(first, SEQ, [(i + 1, i) for i in range(15)]),
    )
    weight, back, back_other, *grads = forward(
        position,
        [own, across, up_own, up_across, down_own, down_across, far],
        (normed, normed_other),
        edges,
        (incoming, upstream_other),
    )

    back_rest = swap(back_other, "core", 2, 1)
    weight_rest = swap(weight, "core", 2, 1)
    along_x = [grads[0]] + [shift(grads[step], "x", 4, step) for step in (1, 3, 2)]
    result = backward(
        (back, back_rest), (weight, weight_rest), inputs, scale_inv, norm_gain[None], incoming
    )
    result, *along_x = join(result, *along_x)

    rows = channels // 16
    by_y = []
    for step in range(4):
        start = ((y + step) % 4) * rows
        parts = [lax.dynamic_slice_in_dim(part, start, rows, axis=1) for part in along_x]
        by_y.append(sum(part.astype(F32) for part in parts))
    total = by_y[0]
    for step in (1, 3, 2):
        total = total + shift(by_y[step].astype(BF16), RING_Y, 4, step).astype(F32)
    weight_grad = share_weight_grad(total, yl, core)
    total_rows = 16 * 16 * count
    return (result[None], weight_grad / math.sqrt(total_rows))


def solution(mesh):
    grid = Mesh(mesh.devices.reshape(SIZES), AXES)
    dp, seq = ("x", "yh", "core"), SEQ
    in_specs = (
        P(dp, seq, None),
        P(dp, seq),
        P(),
        P(),
        P(None, dp, None),
        P(dp, seq, None),
    )
    out_specs = (P(dp, seq, None), P(None, dp, None))
    return jax.shard_map(
        on_device, mesh=grid, in_specs=in_specs, out_specs=out_specs, check_vma=False
    )
```

```python
import functools
import math

import jax
import jax.numpy as jnp
from jax import lax
from jax.experimental import pallas as pl
from jax.experimental.pallas import tpu as pltpu
from jax.sharding import Mesh, PartitionSpec as P

FILTER_TAPS = 3
DILATION_STEP = 32
REACH = 32
AXES = ("x", "yh", "core", "yl", "z")
SIZES = (4, 2, 2, 2, 8)
SEQ = ("yl", "z")
RING_Y = ("yh", "yl")
BF16 = jnp.bfloat16
F32 = jnp.float32


def shift(value, axis, count, step):
    pairs = [(i, (i + step) % count) for i in range(count)]
    return lax.ppermute(value, axis, pairs)


def swap(value, axis, count, mask):
    return lax.ppermute(value, axis, [(i, i ^ mask) for i in range(count)])


def gelu_slope(value):
    coeff = math.sqrt(2.0 / math.pi)
    square = value * value
    tangent = jnp.tanh(value * (coeff + coeff * 0.044715 * square))
    return (0.5 + 0.5 * tangent) * (
        1.0 + value * (1.0 - tangent) * (coeff + coeff * 3.0 * 0.044715 * square)
    )


def join(*arrays):
    return lax.optimization_barrier(arrays)


def load_weight(position, pieces, weight, sem):
    x, yh, core = position[0], position[1], position[2]
    rows = pieces[0].shape[2]
    steps = [(0, 0), (0, 1), (3, 0), (3, 1), (1, 0), (1, 1), (2, 0), (2, 1)]
    blocks = list(pieces[:6]) + [pieces[6].at[0], pieces[6].at[1]]
    copies = []
    for block, (step_x, step_y) in zip(blocks, steps):
        for side in range(2):
            owner = ((x + step_x) % 4) * 4 + ((yh + step_y) % 2) * 2 + (core + side) % 2
            place = pl.multiple_of(owner * rows, 16)
            copies.append(
                pltpu.make_async_copy(
                    block.at[side], weight.at[:, pl.ds(place, rows), :], sem.at[len(copies)]
                )
            )
    return copies


def forward_kernel(position, *refs):
    pieces, refs = refs[:7], refs[7:]
    normed_hbm, edges, upstream_hbm = refs[0:2], refs[2:4], refs[4:6]
    weight_out, back_out, grad_out = refs[6], refs[7:9], refs[9:13]
    weight, normed, upstream, back, grad = refs[13:18]
    piece_sem, load_sem, back_sem, weight_sem, grad_sem = refs[18:]
    x, core = position[0], position[2]
    channels, half = weight.shape[1:]
    count = normed_hbm[0].shape[0]
    lane = pl.multiple_of(core * half, 128)
    copies = load_weight(position, pieces, weight, piece_sem)
    wide = 2 * REACH
    loads = []
    for index in range(2):
        center = upstream_hbm[index]
        if index == 0:
            center = center.at[:, pl.ds(lane, half)]
        rows, lanes = pl.ds(index * wide, wide), pl.ds(index * half, half)
        moves = [
            (normed_hbm[index], normed.at[index, wide : wide + count]),
            (center, upstream.at[index, REACH : REACH + count]),
            (edges[0].at[rows], normed.at[index, :wide]),
            (edges[1].at[rows], normed.at[index, wide + count :]),
            (edges[0].at[2 * wide :, lanes], upstream.at[index, :REACH]),
            (edges[1].at[2 * wide :, lanes], upstream.at[index, REACH + count :]),
        ]
        loads.append(
            [
                pltpu.make_async_copy(source, target, load_sem.at[index, place])
                for place, (source, target) in enumerate(moves)
            ]
        )
    for copy in copies + loads[0]:
        copy.start()
    for copy in copies:
        copy.wait()
    for copy in loads[1]:
        copy.start()
    save = pltpu.make_async_copy(weight, weight_out, weight_sem)
    save.start()
    length = back.shape[1]
    block = length // 3
    wide_lanes = half // 384 * 256
    saves = [save]
    for index in range(2):
        for copy in loads[index]:
            copy.wait()
        narrow = jnp.concatenate([weight[tap, :, wide_lanes:] for tap in range(FILTER_TAPS)], axis=1)
        for start in range(0, length, block):
            conv = jnp.dot(
                normed[index, start : start + block, :],
                weight[0, :, :wide_lanes],
                preferred_element_type=F32,
            )
            for tap in range(1, FILTER_TAPS):
                low = start + tap * DILATION_STEP
                conv = conv + jnp.dot(
                    normed[index, low : low + block, :],
                    weight[tap, :, :wide_lanes],
                    preferred_element_type=F32,
                )
            every = jnp.dot(
                normed[index, start : start + block + wide, :], narrow, preferred_element_type=F32
            )
            lanes_left = half - wide_lanes
            rest = every[:block, :lanes_left]
            for tap in range(1, FILTER_TAPS):
                low = tap * DILATION_STEP
                rest = rest + every[low : low + block, tap * lanes_left : (tap + 1) * lanes_left]
            conv = jnp.concatenate([conv, rest], axis=1)
            incoming = upstream[index, start : start + block, :].astype(F32)
            back[index, start : start + block, :] = (incoming * gelu_slope(conv)).astype(BF16)
        back_save = pltpu.make_async_copy(back.at[index], back_out[index], back_sem.at[index])
        back_save.start()
        saves.append(back_save)
    total = None
    for index in range(2):
        shifted = jnp.concatenate(
            [
                back[index, wide - tap * DILATION_STEP : wide - tap * DILATION_STEP + count, :]
                for tap in range(FILTER_TAPS)
            ],
            axis=1,
        )
        part = lax.dot_general(
            normed[index, wide : wide + count, :],
            shifted,
            (((0,), (0,)), ((), ())),
            preferred_element_type=F32,
        )
        total = part if total is None else total + part
    for tap in range(FILTER_TAPS):
        grad[tap] = total[:, tap * half : (tap + 1) * half].astype(BF16)
    quarter = channels // 4
    for step in range(4):
        place = pl.multiple_of(((x + step) % 4) * quarter, 16)
        grad_save = pltpu.make_async_copy(
            grad.at[:, pl.ds(place, quarter), :], grad_out[step], grad_sem.at[step]
        )
        grad_save.start()
        saves.append(grad_save)
    for copy in saves:
        copy.wait()


def forward(position, pieces, normed, edges, upstream):
    count, channels = normed[0].shape
    half = channels // 2
    length = count + 2 * REACH
    anywhere = pl.BlockSpec(memory_space=pl.ANY)
    dma = pltpu.SemaphoreType.DMA
    return pl.pallas_call(
        forward_kernel,
        out_shape=[jax.ShapeDtypeStruct((FILTER_TAPS, channels, half), BF16)]
        + [jax.ShapeDtypeStruct((length, half), BF16)] * 2
        + [jax.ShapeDtypeStruct((FILTER_TAPS, channels // 4, half), BF16)] * 4,
        in_specs=[pl.BlockSpec(memory_space=pltpu.SMEM)] + [anywhere] * 13,
        out_specs=[anywhere] * 7,
        scratch_shapes=[
            pltpu.VMEM((FILTER_TAPS, channels, half), BF16),
            pltpu.VMEM((2, length + 2 * REACH, channels), BF16),
            pltpu.VMEM((2, length, half), BF16),
            pltpu.VMEM((2, length, half), BF16),
            pltpu.VMEM((FILTER_TAPS, channels, half), BF16),
            dma((16,)),
            dma((2, 6)),
            dma((2,)),
            dma,
            dma((4,)),
        ],
        compiler_params=pltpu.CompilerParams(vmem_limit_bytes=56 * 1024 * 1024),
        name="forward",
    )(position, *pieces, *normed, *edges, *upstream)


def backward_kernel(back_a, back_b, weight_a, weight_b, inputs, scale, gain, incoming, out):
    block = out.shape[0]
    start = pl.program_id(0) * block
    grad = jnp.zeros(out.shape, F32)
    for tap in range(FILTER_TAPS):
        low = pl.multiple_of(start + (FILTER_TAPS - 1 - tap) * DILATION_STEP, 32)
        rows = pl.ds(low, block)
        grad = grad + lax.dot_general(
            jnp.concatenate([back_a[rows, :], back_b[rows, :]], axis=1),
            jnp.concatenate([weight_a[tap], weight_b[tap]], axis=1),
            (((1,), (1,)), ((), ())),
            preferred_element_type=F32,
        )
    scaled = grad * gain[...]
    value = inputs[...]
    factor = scale[...]
    spread = jnp.mean(scaled * value, axis=-1, keepdims=True)
    result = incoming[...].astype(F32) + factor * scaled - value * (factor * factor * factor * spread)
    out[...] = result.astype(BF16)


def backward(back, weight, inputs, scale, gain, incoming):
    count, channels = inputs.shape
    block = 256
    whole = lambda array: pl.BlockSpec(array.shape, lambda i: (0,) * array.ndim)
    part = pl.BlockSpec((block, channels), lambda i: (i, 0))
    return pl.pallas_call(
        backward_kernel,
        grid=(count // block,),
        out_shape=jax.ShapeDtypeStruct((count, channels), BF16),
        in_specs=[whole(back[0]), whole(back[1]), whole(weight[0]), whole(weight[1]), part]
        + [pl.BlockSpec((block, 1), lambda i: (i, 0)), whole(gain), part],
        out_specs=part,
        compiler_params=pltpu.CompilerParams(vmem_limit_bytes=56 * 1024 * 1024),
        name="backward",
    )(*back, *weight, inputs, scale, gain, incoming)


def share_weight_grad(total, yl, core):
    sent = total.astype(BF16)
    near, middle, far = (swap(sent, "z", 8, mask).astype(F32) for mask in (1, 2, 3))
    sent = ((sent.astype(F32) + near) + (middle + far)).astype(BF16)
    mine = (sent.astype(F32) + swap(sent, "z", 8, 7).astype(F32)).astype(BF16)
    pair = ("core", "yl")
    first = lax.ppermute(mine, pair, [(2, 0), (1, 3), (0, 1), (3, 2)])
    second = lax.ppermute(mine, pair, [(2, 1), (1, 2)])
    here = jnp.where(core == yl, mine, first)
    there = jnp.where(core == yl, first, second)
    low = jnp.where(core == 0, here, there)
    high = jnp.where(core == 0, there, here)
    return jnp.concatenate([low, high], axis=2).astype(F32)


def on_device(activations, nucleotides, base_table, norm_gain, filter_weight, upstream):
    x, yh, core, yl = (lax.axis_index(name) for name in ("x", "yh", "core", "yl"))
    y = yh * 2 + yl
    position = jnp.stack([x, yh, core, yl]).astype(jnp.int32)
    tokens, incoming = activations[0], upstream[0]
    count, channels = tokens.shape
    half = channels // 2

    mine = lax.dynamic_slice_in_dim(filter_weight, core * half, half, axis=2)
    other = lax.dynamic_slice_in_dim(filter_weight, (1 - core) * half, half, axis=2)
    own = jnp.stack([mine, swap(other, "core", 2, 1)])
    own, tokens, nucleotides, incoming = join(own, tokens, nucleotides, incoming)

    across = swap(own, RING_Y, 4, 3)
    up_own, down_own = shift(own, "x", 4, 1), shift(own, "x", 4, -1)
    bases = nucleotides[0][:, None]
    row = base_table[3][None]
    for base in (2, 1, 0):
        row = jnp.where(bases == base, base_table[base][None], row)
    inputs = tokens.astype(F32) + row
    scale_inv = lax.rsqrt(jnp.mean(inputs * inputs, axis=-1, keepdims=True) + 1e-06)
    normed = (inputs * scale_inv * norm_gain).astype(BF16)
    own, across, up_own, down_own, normed, incoming = join(
        own, across, up_own, down_own, normed, incoming
    )

    far = shift(jnp.stack([own, across]), "x", 4, 2)
    up_across, down_across = shift(across, "x", 4, 1), shift(across, "x", 4, -1)
    upstream_sent = lax.dynamic_slice_in_dim(incoming, (1 - core) * half, half, axis=1)
    normed_other = swap(normed, "core", 2, 1)
    upstream_other = swap(upstream_sent, "core", 2, 1)
    normed, incoming, normed_other, upstream_other = join(
        normed, incoming, normed_other, upstream_other
    )

    def edge(rows, reach_rows):
        upstream_edge = lax.dynamic_slice_in_dim(incoming[reach_rows], core * half, half, axis=1)
        upstream_edge = jnp.concatenate([upstream_edge, upstream_other[reach_rows]], axis=1)
        return jnp.concatenate([normed[rows], normed_other[rows], upstream_edge])

    last = edge(slice(count - 2 * REACH, count), slice(count - REACH, count))
    first = edge(slice(0, 2 * REACH), slice(0, REACH))
    edges = (
        lax.ppermute(last, SEQ, [(i, i + 1) for i in range(15)]),
        lax.ppermute(first, SEQ, [(i + 1, i) for i in range(15)]),
    )
    weight, back, back_other, *grads = forward(
        position,
        [own, across, up_own, up_across, down_own, down_across, far],
        (normed, normed_other),
        edges,
        (incoming, upstream_other),
    )

    back_rest = swap(back_other, "core", 2, 1)
    weight_rest = swap(weight, "core", 2, 1)
    along_x = [grads[0]] + [shift(grads[step], "x", 4, step) for step in (1, 3, 2)]
    result = backward(
        (back, back_rest), (weight, weight_rest), inputs, scale_inv, norm_gain[None], incoming
    )
    result, *along_x = join(result, *along_x)

    rows = channels // 16
    by_y = []
    for step in range(4):
        start = ((y + step) % 4) * rows
        parts = [lax.dynamic_slice_in_dim(part, start, rows, axis=1) for part in along_x]
        by_y.append(sum(part.astype(F32) for part in parts))
    total = by_y[0]
    for step in (1, 3, 2):
        total = total + shift(by_y[step].astype(BF16), RING_Y, 4, step).astype(F32)
    weight_grad = share_weight_grad(total, yl, core)
    total_rows = 16 * 16 * count
    return (result[None], weight_grad / math.sqrt(total_rows))


def solution(mesh):
    grid = Mesh(mesh.devices.reshape(SIZES), AXES)
    dp, seq = ("x", "yh", "core"), SEQ
    in_specs = (
        P(dp, seq, None),
        P(dp, seq),
        P(),
        P(),
        P(None, dp, None),
        P(dp, seq, None),
    )
    out_specs = (P(dp, seq, None), P(None, dp, None))
    return jax.shard_map(
        on_device, mesh=grid, in_specs=in_specs, out_specs=out_specs, check_vma=False
    )
```

```python
import functools
import math

import jax
import jax.numpy as jnp
from jax import lax
from jax.experimental import pallas as pl
from jax.experimental.pallas import tpu as pltpu
from jax.sharding import Mesh, PartitionSpec as P

FILTER_TAPS = 3
DILATION_STEP = 32
REACH = 32
AXES = ("x", "yh", "core", "yl", "z")
SIZES = (4, 2, 2, 2, 8)
SEQ = ("yl", "z")
RING_Y = ("yh", "yl")
BF16 = jnp.bfloat16
F32 = jnp.float32


def shift(value, axis, count, step):
    pairs = [(i, (i + step) % count) for i in range(count)]
    return lax.ppermute(value, axis, pairs)


def swap(value, axis, count, mask):
    return lax.ppermute(value, axis, [(i, i ^ mask) for i in range(count)])


def gelu_slope(value):
    coeff = math.sqrt(2.0 / math.pi)
    square = value * value
    tangent = jnp.tanh(value * (coeff + coeff * 0.044715 * square))
    return (0.5 + 0.5 * tangent) * (
        1.0 + value * (1.0 - tangent) * (coeff + coeff * 3.0 * 0.044715 * square)
    )


def join(*arrays):
    return lax.optimization_barrier(arrays)


def load_weight(position, pieces, weight, sem):
    x, yh, core = position[0], position[1], position[2]
    rows = pieces[0].shape[2]
    own, across, up, down, far_own, far_across = pieces
    steps = [(0, 0), (0, 1), (3, 0), (3, 1), (1, 0), (1, 1), (2, 0), (2, 1)]
    blocks = [own, across, up.at[0], up.at[1], down.at[0], down.at[1], far_own, far_across]
    copies = []
    for block, (step_x, step_y) in zip(blocks, steps):
        for side in range(2):
            owner = ((x + step_x) % 4) * 4 + ((yh + step_y) % 2) * 2 + (core + side) % 2
            place = pl.multiple_of(owner * rows, 16)
            copies.append(
                pltpu.make_async_copy(
                    block.at[side], weight.at[:, pl.ds(place, rows), :], sem.at[len(copies)]
                )
            )
    return copies


def forward_kernel(position, *refs):
    pieces, refs = refs[:6], refs[6:]
    normed_hbm, edges, upstream_hbm = refs[0:2], refs[2:4], refs[4:6]
    weight_out, back_out, grad_out = refs[6], refs[7:9], refs[9:13]
    weight, normed, upstream, back, grad = refs[13:18]
    piece_sem, load_sem, back_sem, weight_sem, grad_sem = refs[18:]
    x, core = position[0], position[2]
    channels, half = weight.shape[1:]
    count = normed_hbm[0].shape[0]
    lane = pl.multiple_of(core * half, 128)
    copies = load_weight(position, pieces, weight, piece_sem)
    wide = 2 * REACH
    loads = []
    for index in range(2):
        center = upstream_hbm[index]
        if index == 0:
            center = center.at[:, pl.ds(lane, half)]
        rows, lanes = pl.ds(index * wide, wide), pl.ds(index * half, half)
        moves = [
            (normed_hbm[index], normed.at[index, wide : wide + count]),
            (center, upstream.at[index, REACH : REACH + count]),
            (edges[0].at[rows], normed.at[index, :wide]),
            (edges[1].at[rows], normed.at[index, wide + count :]),
            (edges[0].at[2 * wide :, lanes], upstream.at[index, :REACH]),
            (edges[1].at[2 * wide :, lanes], upstream.at[index, REACH + count :]),
        ]
        loads.append(
            [
                pltpu.make_async_copy(source, target, load_sem.at[index, place])
                for place, (source, target) in enumerate(moves)
            ]
        )
    for copy in copies + loads[0]:
        copy.start()
    for copy in copies:
        copy.wait()
    for copy in loads[1]:
        copy.start()
    save = pltpu.make_async_copy(weight, weight_out, weight_sem)
    save.start()
    length = back.shape[1]
    block = length // 3
    wide_lanes = half // 384 * 256
    saves = [save]
    for index in range(2):
        for copy in loads[index]:
            copy.wait()
        narrow = jnp.concatenate([weight[tap, :, wide_lanes:] for tap in range(FILTER_TAPS)], axis=1)
        for start in range(0, length, block):
            conv = jnp.dot(
                normed[index, start : start + block, :],
                weight[0, :, :wide_lanes],
                preferred_element_type=F32,
            )
            for tap in range(1, FILTER_TAPS):
                low = start + tap * DILATION_STEP
                conv = conv + jnp.dot(
                    normed[index, low : low + block, :],
                    weight[tap, :, :wide_lanes],
                    preferred_element_type=F32,
                )
            every = jnp.dot(
                normed[index, start : start + block + wide, :], narrow, preferred_element_type=F32
            )
            lanes_left = half - wide_lanes
            rest = every[:block, :lanes_left]
            for tap in range(1, FILTER_TAPS):
                low = tap * DILATION_STEP
                rest = rest + every[low : low + block, tap * lanes_left : (tap + 1) * lanes_left]
            conv = jnp.concatenate([conv, rest], axis=1)
            incoming = upstream[index, start : start + block, :].astype(F32)
            back[index, start : start + block, :] = (incoming * gelu_slope(conv)).astype(BF16)
        back_save = pltpu.make_async_copy(back.at[index], back_out[index], back_sem.at[index])
        back_save.start()
        saves.append(back_save)
    total = None
    for index in range(2):
        shifted = jnp.concatenate(
            [
                back[index, wide - tap * DILATION_STEP : wide - tap * DILATION_STEP + count, :]
                for tap in range(FILTER_TAPS)
            ],
            axis=1,
        )
        part = lax.dot_general(
            normed[index, wide : wide + count, :],
            shifted,
            (((0,), (0,)), ((), ())),
            preferred_element_type=F32,
        )
        total = part if total is None else total + part
    for tap in range(FILTER_TAPS):
        grad[tap] = total[:, tap * half : (tap + 1) * half].astype(BF16)
    quarter = channels // 4
    for step in range(4):
        place = pl.multiple_of(((x + step) % 4) * quarter, 16)
        grad_save = pltpu.make_async_copy(
            grad.at[:, pl.ds(place, quarter), :], grad_out[step], grad_sem.at[step]
        )
        grad_save.start()
        saves.append(grad_save)
    for copy in saves:
        copy.wait()


def forward(position, pieces, normed, edges, upstream):
    count, channels = normed[0].shape
    half = channels // 2
    length = count + 2 * REACH
    anywhere = pl.BlockSpec(memory_space=pl.ANY)
    dma = pltpu.SemaphoreType.DMA
    return pl.pallas_call(
        forward_kernel,
        out_shape=[jax.ShapeDtypeStruct((FILTER_TAPS, channels, half), BF16)]
        + [jax.ShapeDtypeStruct((length, half), BF16)] * 2
        + [jax.ShapeDtypeStruct((FILTER_TAPS, channels // 4, half), BF16)] * 4,
        in_specs=[pl.BlockSpec(memory_space=pltpu.SMEM)] + [anywhere] * 12,
        out_specs=[anywhere] * 7,
        scratch_shapes=[
            pltpu.VMEM((FILTER_TAPS, channels, half), BF16),
            pltpu.VMEM((2, length + 2 * REACH, channels), BF16),
            pltpu.VMEM((2, length, half), BF16),
            pltpu.VMEM((2, length, half), BF16),
            pltpu.VMEM((FILTER_TAPS, channels, half), BF16),
            dma((16,)),
            dma((2, 6)),
            dma((2,)),
            dma,
            dma((4,)),
        ],
        compiler_params=pltpu.CompilerParams(vmem_limit_bytes=56 * 1024 * 1024),
        name="forward",
    )(position, *pieces, *normed, *edges, *upstream)


def backward_kernel(back_a, back_b, weight_a, weight_b, inputs, scale, gain, incoming, out):
    block = out.shape[0]
    start = pl.program_id(0) * block
    grad = jnp.zeros(out.shape, F32)
    for tap in range(FILTER_TAPS):
        low = pl.multiple_of(start + (FILTER_TAPS - 1 - tap) * DILATION_STEP, 32)
        rows = pl.ds(low, block)
        grad = grad + lax.dot_general(
            jnp.concatenate([back_a[rows, :], back_b[rows, :]], axis=1),
            jnp.concatenate([weight_a[tap], weight_b[tap]], axis=1),
            (((1,), (1,)), ((), ())),
            preferred_element_type=F32,
        )
    scaled = grad * gain[...]
    value = inputs[...]
    factor = scale[...]
    spread = jnp.mean(scaled * value, axis=-1, keepdims=True)
    result = incoming[...].astype(F32) + factor * scaled - value * (factor * factor * factor * spread)
    out[...] = result.astype(BF16)


def backward(back, weight, inputs, scale, gain, incoming):
    count, channels = inputs.shape
    block = 256
    whole = lambda array: pl.BlockSpec(array.shape, lambda i: (0,) * array.ndim)
    part = pl.BlockSpec((block, channels), lambda i: (i, 0))
    return pl.pallas_call(
        backward_kernel,
        grid=(count // block,),
        out_shape=jax.ShapeDtypeStruct((count, channels), BF16),
        in_specs=[whole(back[0]), whole(back[1]), whole(weight[0]), whole(weight[1]), part]
        + [pl.BlockSpec((block, 1), lambda i: (i, 0)), whole(gain), part],
        out_specs=part,
        compiler_params=pltpu.CompilerParams(vmem_limit_bytes=36 * 1024 * 1024),
        name="backward",
    )(*back, *weight, inputs, scale, gain, incoming)


def share_weight_grad(total, yl, core):
    sent = total.astype(BF16)
    near, middle, far = (swap(sent, "z", 8, mask).astype(F32) for mask in (1, 2, 3))
    sent = ((sent.astype(F32) + near) + (middle + far)).astype(BF16)
    mine = (sent.astype(F32) + swap(sent, "z", 8, 7).astype(F32)).astype(BF16)
    pair = ("core", "yl")
    first = lax.ppermute(mine, pair, [(2, 0), (1, 3), (0, 1), (3, 2)])
    second = lax.ppermute(mine, pair, [(2, 1), (1, 2)])
    here = jnp.where(core == yl, mine, first)
    there = jnp.where(core == yl, first, second)
    low = jnp.where(core == 0, here, there)
    high = jnp.where(core == 0, there, here)
    return jnp.concatenate([low, high], axis=2).astype(F32)


def on_device(activations, nucleotides, base_table, norm_gain, filter_weight, upstream):
    x, yh, core, yl = (lax.axis_index(name) for name in ("x", "yh", "core", "yl"))
    y = yh * 2 + yl
    position = jnp.stack([x, yh, core, yl]).astype(jnp.int32)
    tokens, incoming = activations[0], upstream[0]
    count, channels = tokens.shape
    half = channels // 2

    mine = lax.dynamic_slice_in_dim(filter_weight, core * half, half, axis=2)
    other = lax.dynamic_slice_in_dim(filter_weight, (1 - core) * half, half, axis=2)
    own = jnp.stack([mine, swap(other, "core", 2, 1)])
    own, tokens, nucleotides, incoming = join(own, tokens, nucleotides, incoming)

    across = swap(own, RING_Y, 4, 3)
    far_own = shift(own, "x", 4, 2)
    hot = (nucleotides[0][:, None] == jnp.arange(4, dtype=jnp.int32)[None, :]).astype(F32)
    inputs = tokens.astype(F32) + jnp.dot(hot, base_table, precision=lax.Precision.HIGHEST)
    scale_inv = lax.rsqrt(jnp.mean(inputs * inputs, axis=-1, keepdims=True) + 1e-06)
    normed = (inputs * scale_inv * norm_gain).astype(BF16)
    own, across, far_own, normed, incoming = join(own, across, far_own, normed, incoming)

    pair = jnp.stack([own, across])
    up, down = shift(pair, "x", 4, 1), shift(pair, "x", 4, -1)
    far_across = shift(across, "x", 4, 2)
    upstream_sent = lax.dynamic_slice_in_dim(incoming, (1 - core) * half, half, axis=1)
    normed_other = swap(normed, "core", 2, 1)
    upstream_other = swap(upstream_sent, "core", 2, 1)
    normed, incoming, normed_other, upstream_other = join(
        normed, incoming, normed_other, upstream_other
    )

    def edge(rows, reach_rows):
        upstream_edge = lax.dynamic_slice_in_dim(incoming[reach_rows], core * half, half, axis=1)
        upstream_edge = jnp.concatenate([upstream_edge, upstream_other[reach_rows]], axis=1)
        return jnp.concatenate([normed[rows], normed_other[rows], upstream_edge])

    last = edge(slice(count - 2 * REACH, count), slice(count - REACH, count))
    first = edge(slice(0, 2 * REACH), slice(0, REACH))
    edges = (
        lax.ppermute(last, SEQ, [(i, i + 1) for i in range(15)]),
        lax.ppermute(first, SEQ, [(i + 1, i) for i in range(15)]),
    )
    weight, back, back_other, *grads = forward(
        position,
        [own, across, up, down, far_own, far_across],
        (normed, normed_other),
        edges,
        (incoming, upstream_other),
    )

    back_rest = swap(back_other, "core", 2, 1)
    weight_rest = swap(weight, "core", 2, 1)
    along_x = [grads[0]] + [shift(grads[step], "x", 4, step) for step in (1, 3, 2)]
    result = backward(
        (back, back_rest), (weight, weight_rest), inputs, scale_inv, norm_gain[None], incoming
    )
    result, *along_x = join(result, *along_x)

    rows = channels // 16
    by_y = []
    for step in range(4):
        start = ((y + step) % 4) * rows
        parts = [lax.dynamic_slice_in_dim(part, start, rows, axis=1) for part in along_x]
        by_y.append(sum(part.astype(F32) for part in parts))
    total = by_y[0]
    for step in (1, 3, 2):
        total = total + shift(by_y[step].astype(BF16), RING_Y, 4, step).astype(F32)
    weight_grad = share_weight_grad(total, yl, core)
    total_rows = 16 * 16 * count
    return (result[None], weight_grad / math.sqrt(total_rows))


def solution(mesh):
    grid = Mesh(mesh.devices.reshape(SIZES), AXES)
    dp, seq = ("x", "yh", "core"), SEQ
    in_specs = (
        P(dp, seq, None),
        P(dp, seq),
        P(),
        P(),
        P(None, dp, None),
        P(dp, seq, None),
    )
    out_specs = (P(dp, seq, None), P(None, dp, None))
    return jax.shard_map(
        on_device, mesh=grid, in_specs=in_specs, out_specs=out_specs, check_vma=False
    )
```

```python
import functools
import math

import jax
import jax.numpy as jnp
from jax import lax
from jax.experimental import pallas as pl
from jax.experimental.pallas import tpu as pltpu
from jax.sharding import Mesh, PartitionSpec as P

FILTER_TAPS = 3
DILATION_STEP = 32
REACH = 32
AXES = ("x", "yh", "core", "yl", "z")
SIZES = (4, 2, 2, 2, 8)
SEQ = ("yl", "z")
RING_Y = ("yh", "yl")
BF16 = jnp.bfloat16
F32 = jnp.float32


def shift(value, axis, count, step):
    pairs = [(i, (i + step) % count) for i in range(count)]
    return lax.ppermute(value, axis, pairs)


def swap(value, axis, count, mask):
    return lax.ppermute(value, axis, [(i, i ^ mask) for i in range(count)])


def gelu_slope(value):
    coeff = math.sqrt(2.0 / math.pi)
    square = value * value
    tangent = jnp.tanh(value * (coeff + coeff * 0.044715 * square))
    return (0.5 + 0.5 * tangent) * (
        1.0 + value * (1.0 - tangent) * (coeff + coeff * 3.0 * 0.044715 * square)
    )


def join(*arrays):
    return lax.optimization_barrier(arrays)


def load_weight(position, pieces, weight, sem):
    x, yh, core = position[0], position[1], position[2]
    rows = pieces[0].shape[2]
    own, across, up, down, far_own, far_across = pieces
    steps = [(0, 0), (0, 1), (3, 0), (3, 1), (1, 0), (1, 1), (2, 0), (2, 1)]
    blocks = [own, across, up.at[0], up.at[1], down.at[0], down.at[1], far_own, far_across]
    copies = []
    for block, (step_x, step_y) in zip(blocks, steps):
        for side in range(2):
            owner = ((x + step_x) % 4) * 4 + ((yh + step_y) % 2) * 2 + (core + side) % 2
            place = pl.multiple_of(owner * rows, 16)
            copies.append(
                pltpu.make_async_copy(
                    block.at[side], weight.at[:, pl.ds(place, rows), :], sem.at[len(copies)]
                )
            )
    return copies


def forward_kernel(position, *refs):
    pieces, refs = refs[:6], refs[6:]
    normed_hbm, edges, upstream_hbm = refs[0:2], refs[2:4], refs[4:6]
    weight_out, back_out, grad_out = refs[6], refs[7:9], refs[9:13]
    weight, normed, upstream, back, grad = refs[13:18]
    piece_sem, load_sem, back_sem, weight_sem, grad_sem = refs[18:]
    x, core = position[0], position[2]
    channels, half = weight.shape[1:]
    count = normed_hbm[0].shape[0]
    lane = pl.multiple_of(core * half, 128)
    copies = load_weight(position, pieces, weight, piece_sem)
    wide = 2 * REACH
    loads = []
    for index in range(2):
        center = upstream_hbm[index]
        if index == 0:
            center = center.at[:, pl.ds(lane, half)]
        rows, lanes = pl.ds(index * wide, wide), pl.ds(index * half, half)
        moves = [
            (normed_hbm[index], normed.at[index, wide : wide + count]),
            (center, upstream.at[index, REACH : REACH + count]),
            (edges[0].at[rows], normed.at[index, :wide]),
            (edges[1].at[rows], normed.at[index, wide + count :]),
            (edges[0].at[2 * wide :, lanes], upstream.at[index, :REACH]),
            (edges[1].at[2 * wide :, lanes], upstream.at[index, REACH + count :]),
        ]
        loads.append(
            [
                pltpu.make_async_copy(source, target, load_sem.at[index, place])
                for place, (source, target) in enumerate(moves)
            ]
        )
    for copy in copies + loads[0]:
        copy.start()
    for copy in copies:
        copy.wait()
    for copy in loads[1]:
        copy.start()
    save = pltpu.make_async_copy(weight, weight_out, weight_sem)
    save.start()
    length = back.shape[1]
    block = length // 3
    wide_lanes = half // 384 * 256
    saves = [save]
    for index in range(2):
        for copy in loads[index]:
            copy.wait()
        narrow = jnp.concatenate([weight[tap, :, wide_lanes:] for tap in range(FILTER_TAPS)], axis=1)
        for start in range(0, length, block):
            conv = jnp.dot(
                normed[index, start : start + block, :],
                weight[0, :, :wide_lanes],
                preferred_element_type=F32,
            )
            for tap in range(1, FILTER_TAPS):
                low = start + tap * DILATION_STEP
                conv = conv + jnp.dot(
                    normed[index, low : low + block, :],
                    weight[tap, :, :wide_lanes],
                    preferred_element_type=F32,
                )
            every = jnp.dot(
                normed[index, start : start + block + wide, :], narrow, preferred_element_type=F32
            )
            lanes_left = half - wide_lanes
            rest = every[:block, :lanes_left]
            for tap in range(1, FILTER_TAPS):
                low = tap * DILATION_STEP
                rest = rest + every[low : low + block, tap * lanes_left : (tap + 1) * lanes_left]
            conv = jnp.concatenate([conv, rest], axis=1)
            incoming = upstream[index, start : start + block, :].astype(F32)
            back[index, start : start + block, :] = (incoming * gelu_slope(conv)).astype(BF16)
        back_save = pltpu.make_async_copy(back.at[index], back_out[index], back_sem.at[index])
        back_save.start()
        saves.append(back_save)
    total = None
    for index in range(2):
        shifted = jnp.concatenate(
            [
                back[index, wide - tap * DILATION_STEP : wide - tap * DILATION_STEP + count, :]
                for tap in range(FILTER_TAPS)
            ],
            axis=1,
        )
        part = lax.dot_general(
            normed[index, wide : wide + count, :],
            shifted,
            (((0,), (0,)), ((), ())),
            preferred_element_type=F32,
        )
        total = part if total is None else total + part
    quarter = channels // 4
    for tap in range(FILTER_TAPS):
        grad[tap] = total[:, tap * half : (tap + 1) * half].astype(BF16)
        for step in range(4):
            place = pl.multiple_of(((x + step) % 4) * quarter, 16)
            grad_save = pltpu.make_async_copy(
                grad.at[tap, pl.ds(place, quarter), :],
                grad_out[step].at[tap],
                grad_sem.at[tap, step],
            )
            grad_save.start()
            saves.append(grad_save)
    for copy in saves:
        copy.wait()


def forward(position, pieces, normed, edges, upstream):
    count, channels = normed[0].shape
    half = channels // 2
    length = count + 2 * REACH
    anywhere = pl.BlockSpec(memory_space=pl.ANY)
    dma = pltpu.SemaphoreType.DMA
    return pl.pallas_call(
        forward_kernel,
        out_shape=[jax.ShapeDtypeStruct((FILTER_TAPS, channels, half), BF16)]
        + [jax.ShapeDtypeStruct((length, half), BF16)] * 2
        + [jax.ShapeDtypeStruct((FILTER_TAPS, channels // 4, half), BF16)] * 4,
        in_specs=[pl.BlockSpec(memory_space=pltpu.SMEM)] + [anywhere] * 12,
        out_specs=[anywhere] * 7,
        scratch_shapes=[
            pltpu.VMEM((FILTER_TAPS, channels, half), BF16),
            pltpu.VMEM((2, length + 2 * REACH, channels), BF16),
            pltpu.VMEM((2, length, half), BF16),
            pltpu.VMEM((2, length, half), BF16),
            pltpu.VMEM((FILTER_TAPS, channels, half), BF16),
            dma((16,)),
            dma((2, 6)),
            dma((2,)),
            dma,
            dma((FILTER_TAPS, 4)),
        ],
        compiler_params=pltpu.CompilerParams(vmem_limit_bytes=56 * 1024 * 1024),
        name="forward",
    )(position, *pieces, *normed, *edges, *upstream)


def backward_kernel(back_a, back_b, weight_a, weight_b, inputs, scale, gain, incoming, out):
    block = out.shape[0]
    start = pl.program_id(0) * block
    grad = jnp.zeros(out.shape, F32)
    for tap in range(FILTER_TAPS):
        low = pl.multiple_of(start + (FILTER_TAPS - 1 - tap) * DILATION_STEP, 32)
        rows = pl.ds(low, block)
        grad = grad + lax.dot_general(
            jnp.concatenate([back_a[rows, :], back_b[rows, :]], axis=1),
            jnp.concatenate([weight_a[tap], weight_b[tap]], axis=1),
            (((1,), (1,)), ((), ())),
            preferred_element_type=F32,
        )
    scaled = grad * gain[...]
    value = inputs[...]
    factor = scale[...]
    spread = jnp.mean(scaled * value, axis=-1, keepdims=True)
    result = incoming[...].astype(F32) + factor * scaled - value * (factor * factor * factor * spread)
    out[...] = result.astype(BF16)


def backward(back, weight, inputs, scale, gain, incoming):
    count, channels = inputs.shape
    block = 320
    whole = lambda array: pl.BlockSpec(array.shape, lambda i: (0,) * array.ndim)
    part = pl.BlockSpec((block, channels), lambda i: (i, 0))
    return pl.pallas_call(
        backward_kernel,
        grid=(count // block,),
        out_shape=jax.ShapeDtypeStruct((count, channels), BF16),
        in_specs=[whole(back[0]), whole(back[1]), whole(weight[0]), whole(weight[1]), part]
        + [pl.BlockSpec((block, 1), lambda i: (i, 0)), whole(gain), part],
        out_specs=part,
        compiler_params=pltpu.CompilerParams(vmem_limit_bytes=36 * 1024 * 1024),
        name="backward",
    )(*back, *weight, inputs, scale, gain, incoming)


def share_weight_grad(total, yl, core):
    sent = total.astype(BF16)
    near, middle, far = (swap(sent, "z", 8, mask).astype(F32) for mask in (1, 2, 3))
    sent = ((sent.astype(F32) + near) + (middle + far)).astype(BF16)
    mine = (sent.astype(F32) + swap(sent, "z", 8, 7).astype(F32)).astype(BF16)
    pair = ("core", "yl")
    first = lax.ppermute(mine, pair, [(2, 0), (1, 3), (0, 1), (3, 2)])
    second = lax.ppermute(mine, pair, [(2, 1), (1, 2)])
    here = jnp.where(core == yl, mine, first)
    there = jnp.where(core == yl, first, second)
    low = jnp.where(core == 0, here, there)
    high = jnp.where(core == 0, there, here)
    return jnp.concatenate([low, high], axis=2).astype(F32)


def on_device(activations, nucleotides, base_table, norm_gain, filter_weight, upstream):
    x, yh, core, yl = (lax.axis_index(name) for name in ("x", "yh", "core", "yl"))
    y = yh * 2 + yl
    position = jnp.stack([x, yh, core, yl]).astype(jnp.int32)
    tokens, incoming = activations[0], upstream[0]
    count, channels = tokens.shape
    half = channels // 2

    mine = lax.dynamic_slice_in_dim(filter_weight, core * half, half, axis=2)
    other = lax.dynamic_slice_in_dim(filter_weight, (1 - core) * half, half, axis=2)
    own = jnp.stack([mine, swap(other, "core", 2, 1)])
    own, tokens, nucleotides, incoming = join(own, tokens, nucleotides, incoming)

    across = swap(own, RING_Y, 4, 3)
    far_own = shift(own, "x", 4, 2)
    hot = (nucleotides[0][:, None] == jnp.arange(4, dtype=jnp.int32)[None, :]).astype(F32)
    inputs = tokens.astype(F32) + jnp.dot(hot, base_table, precision=lax.Precision.HIGHEST)
    scale_inv = lax.rsqrt(jnp.mean(inputs * inputs, axis=-1, keepdims=True) + 1e-06)
    normed = (inputs * scale_inv * norm_gain).astype(BF16)
    own, across, far_own, normed, incoming = join(own, across, far_own, normed, incoming)

    pair = jnp.stack([own, across])
    up, down = shift(pair, "x", 4, 1), shift(pair, "x", 4, -1)
    far_across = shift(across, "x", 4, 2)
    upstream_sent = lax.dynamic_slice_in_dim(incoming, (1 - core) * half, half, axis=1)
    normed_other = swap(normed, "core", 2, 1)
    upstream_other = swap(upstream_sent, "core", 2, 1)
    normed, incoming, normed_other, upstream_other = join(
        normed, incoming, normed_other, upstream_other
    )

    def edge(rows, reach_rows):
        upstream_edge = lax.dynamic_slice_in_dim(incoming[reach_rows], core * half, half, axis=1)
        upstream_edge = jnp.concatenate([upstream_edge, upstream_other[reach_rows]], axis=1)
        return jnp.concatenate([normed[rows], normed_other[rows], upstream_edge])

    last = edge(slice(count - 2 * REACH, count), slice(count - REACH, count))
    first = edge(slice(0, 2 * REACH), slice(0, REACH))
    edges = (
        lax.ppermute(last, SEQ, [(i, i + 1) for i in range(15)]),
        lax.ppermute(first, SEQ, [(i + 1, i) for i in range(15)]),
    )
    weight, back, back_other, *grads = forward(
        position,
        [own, across, up, down, far_own, far_across],
        (normed, normed_other),
        edges,
        (incoming, upstream_other),
    )

    back_rest = swap(back_other, "core", 2, 1)
    weight_rest = swap(weight, "core", 2, 1)
    along_x = [grads[0]] + [shift(grads[step], "x", 4, step) for step in (1, 3, 2)]
    result = backward(
        (back, back_rest), (weight, weight_rest), inputs, scale_inv, norm_gain[None], incoming
    )
    result, *along_x = join(result, *along_x)

    rows = channels // 16
    by_y = []
    for step in range(4):
        start = ((y + step) % 4) * rows
        parts = [lax.dynamic_slice_in_dim(part, start, rows, axis=1) for part in along_x]
        by_y.append(sum(part.astype(F32) for part in parts))
    total = by_y[0]
    for step in (1, 3, 2):
        total = total + shift(by_y[step].astype(BF16), RING_Y, 4, step).astype(F32)
    weight_grad = share_weight_grad(total, yl, core)
    total_rows = 16 * 16 * count
    return (result[None], weight_grad / math.sqrt(total_rows))


def solution(mesh):
    grid = Mesh(mesh.devices.reshape(SIZES), AXES)
    dp, seq = ("x", "yh", "core"), SEQ
    in_specs = (
        P(dp, seq, None),
        P(dp, seq),
        P(),
        P(),
        P(None, dp, None),
        P(dp, seq, None),
    )
    out_specs = (P(dp, seq, None), P(None, dp, None))
    return jax.shard_map(
        on_device, mesh=grid, in_specs=in_specs, out_specs=out_specs, check_vma=False
    )
```
